256 devices in a mesh: cluster: 32 (over y, z), sub: 8 (over x, core).
Axes of the slice: x: 4, y: 4, z: 8, core: 2. Of those that a mesh axis runs over, the one named last changes fastest.
Arguments:
- right_side: float32 [8, 32, 16, 384], P('sub', 'cluster'), may hold values from -12 to 12
- schur: float32 [8, 32, 768, 768], P('sub', 'cluster'), as said below
- rigid_modes: float32 [8, 32, 6, 768], P('sub', 'cluster'), may hold values from -0.21875 to 0.21875
- mode_count: int32 [8, 32], P('sub', 'cluster'), may hold values from 3 to 6
- face_order: int32 [8, 32, 384], P('sub', 'cluster'), may hold values from 0 to 383, each once within a row
- dual_scale: float32 [8, 32, 384], P('sub', 'cluster'), may hold values from 0.5 to 2
- rigid_loads: float32 [8, 32, 6, 16], P('sub', 'cluster'), may hold values from -6 to 6
- coarse_inverse: float32 [1536, 1536], P(('cluster', 'sub')), as said below
Outputs:
- multipliers: float32 [8, 32, 16, 384], P('sub', 'cluster')
- residual: float32 [8, 32, 16, 384], P('sub', 'cluster')
The draws below stay inside these ranges and needn't reach their ends.
Inputs may be any that keep to these rules, and one draw needn't show every extreme that they name: rigid-body modes m with m >= mode_count are unused. `face_order`: each subdomain's entries form a permutation of the face unknowns; those of the first subdomain of a chain are unused. `schur`: each subdomain's matrix is symmetric. `coarse_inverse`: symmetric.
All inputs are finite; a program needn't handle non-finite values.
Results may differ from the reference program's by a relative error of at most 0.0003.
Values sent between devices are 32-bit elements; how exact they have to be, the bound alone decides.
A program may use at most 64 MiB of HBM per device.

```python
import math
import jax
import jax.numpy as jnp
from jax import lax

NI = 768
M = 384
CASES = 16
MODES = 6
ITERS = 2
SUB_DEV = 1
CHAIN = 32
NC = 1536
N_CLUSTER = 32
N_SUB = 8


def draw_schur(key, part):

    def single_matrix(matrix_index):
        sub_key = jax.random.fold_in(key, matrix_index)
        random_part = jax.random.normal(sub_key, (NI, NI), jnp.float32)
        symmetric = (random_part + random_part.T) * (0.5 / jnp.sqrt(2.0 * NI))
        return symmetric + 2.0 * jnp.eye(NI, dtype=jnp.float32)
    matrices = lax.map(single_matrix, jnp.arange(N_SUB * CHAIN))
    return matrices.reshape(N_SUB, CHAIN, NI, NI)


def draw_coarse_inverse(key, part):
    random_part = jax.random.normal(key, (NC, NC), jnp.float32)
    return jnp.eye(NC, dtype=jnp.float32) + (random_part + random_part.T) * (0.5 / jnp.sqrt(2.0 * NC))


def draw_right_side(key, part):
    growth = 1.0 + 2.0 * jnp.arange(CHAIN, dtype=jnp.float32) / max(CHAIN - 1, 1)
    growth = growth[None, :, None, None]
    random_part = jnp.clip(jax.random.normal(key, (N_SUB, CHAIN, CASES, M), jnp.float32), -4.0, 4.0)
    return random_part * growth


def plant(values, stream_key, smallest, largest):
    extent = values.shape
    index_at = [jax.random.randint(jax.random.fold_in(stream_key, axis), (), 0, extent[axis]) for axis in range(len(extent))]
    values = values.at[tuple(index_at)].set(smallest)
    longest = extent.index(max(extent))
    index_at[longest] = (index_at[longest] + 1) % extent[longest]
    return values.at[tuple(index_at)].set(largest)


def block_scale(own_key, dims, pieces, low, high):
    def one(position, blocks):
        steps = jax.random.uniform(jax.random.fold_in(jax.random.fold_in(own_key, 6), position), (blocks,), jnp.float32, low / len(pieces), high / len(pieces))
        return jnp.repeat(jnp.exp(steps), dims[position] // blocks).reshape((-1,) + (1,) * (len(dims) - position - 1))

    loudness = one(*pieces[0])
    for cut in pieces[1:]:
        loudness = loudness * one(*cut)
    return loudness


def centred(stream_key, dims, deviation, bound, shards=(), kind=jnp.bfloat16):
    loudness = block_scale(stream_key, dims, shards, -0.22, 0.18) if shards else 1.0
    drawn = jax.random.normal(stream_key, dims, jnp.float32) * deviation * loudness
    return jnp.minimum(jnp.maximum(drawn, -bound), bound).astype(kind)


def setup_inputs(seed: int = 0) -> dict:
    arg_keys = jax.random.split(jax.random.key(seed), 9)
    return {
        "right_side": draw_right_side(jax.random.fold_in(arg_keys[8], 71), 0),
        "schur": draw_schur(jax.random.fold_in(arg_keys[8], 71), 0),
        "rigid_modes": centred(arg_keys[2], (N_SUB, CHAIN, MODES, NI), NI ** -0.5, 0.21875, ((0, 8), (1, 32)), jnp.float32),
        "mode_count": plant(jax.random.randint(arg_keys[3], (N_SUB, CHAIN), 3, 7), jax.random.fold_in(arg_keys[3], 1), 3, 6).astype(jnp.int32),
        "face_order": jax.vmap(lambda own: jax.random.permutation(own, M))(jax.random.split(arg_keys[4], N_SUB * CHAIN)).reshape((N_SUB, CHAIN, M)).astype(jnp.int32),
        "dual_scale": jnp.clip(jnp.exp(math.log(2.0) - 1.3862944 * jax.random.uniform(arg_keys[5], (N_SUB, CHAIN, M), jnp.float32) ** block_scale(arg_keys[5], (N_SUB, CHAIN, M), ((0, 8), (1, 32)), -0.2, 0.2)), 0.5, 2.0),
        "rigid_loads": centred(arg_keys[6], (N_SUB, CHAIN, MODES, CASES), 1.0, 6.0, ((0, 8), (1, 32)), jnp.float32),
        "coarse_inverse": draw_coarse_inverse(jax.random.fold_in(arg_keys[8], 71), 0),
    }


highest = lax.Precision.HIGHEST

def lift_faces(dual_field, face_order):
    earlier = jnp.concatenate([jnp.zeros_like(dual_field[:, :1]), dual_field[:, :-1]], axis=1)
    gather_index = jnp.broadcast_to(face_order[:, :, None, :], earlier.shape)
    left_face = -jnp.take_along_axis(earlier, gather_index, axis=3)
    return jnp.concatenate([left_face, dual_field], axis=3)

def push_faces(values, inverse):
    half_size = values.shape[3] // 2
    left_face = values[..., :half_size]
    right_face = values[..., half_size:]
    gather_index = jnp.broadcast_to(inverse[:, :, None, :], left_face.shape)
    returned = -jnp.take_along_axis(left_face, gather_index, axis=3)
    following = jnp.concatenate([returned[:, 1:], jnp.zeros_like(returned[:, :1])], axis=1)
    return right_face + following

def apply_dual(dual_field, schur, face_order, inverse):
    lifted = lift_faces(dual_field, face_order)
    dual_image = jnp.einsum('sjci,sjik->sjck', lifted, schur, precision=highest)
    return push_faces(dual_image, inverse)

def basis_transpose(dual_field, basis, face_order):
    return jnp.einsum('sjmi,sjci->sjmc', basis, lift_faces(dual_field, face_order), precision=highest)

def basis_expand(coefficients, basis, inverse):
    return push_faces(jnp.einsum('sjmi,sjmc->sjci', basis, coefficients, precision=highest), inverse)

def coarse_solve(coefficients, coarse_inverse):
    flattened = coefficients.reshape(N_SUB, N_CLUSTER, SUB_DEV, MODES, CASES).transpose(1, 0, 2, 3, 4).reshape(NC, CASES)
    solved = jnp.dot(coarse_inverse, flattened, precision=highest)
    return solved.reshape(N_CLUSTER, N_SUB, SUB_DEV, MODES, CASES).transpose(1, 0, 2, 3, 4).reshape(N_SUB, CHAIN, MODES, CASES)

def project(dual_field, basis, face_order, inverse, coarse_inverse):
    coefficients = basis_transpose(dual_field, basis, face_order)
    return dual_field - basis_expand(coarse_solve(coefficients, coarse_inverse), basis, inverse)

def gram_product(first_field, second_field):
    return jnp.einsum('sjcm,sjdm->cd', first_field, second_field, precision=highest)

def solve_small(matrix, right_hand):
    factor = jnp.linalg.cholesky(matrix)
    halfway = lax.linalg.triangular_solve(factor, right_hand, left_side=True, lower=True)
    return lax.linalg.triangular_solve(factor, halfway, left_side=True, lower=True, transpose_a=True)

def reference(right_side, schur, rigid_modes, mode_count, face_order, dual_scale, rigid_loads, coarse_inverse):
    inverse = jnp.argsort(face_order, axis=-1).astype(jnp.int32)
    active = (jnp.arange(MODES)[None, None, :] < mode_count[:, :, None]).astype(jnp.float32)
    basis = rigid_modes * active[..., None]
    masked_loads = rigid_loads * active[..., None]
    scaling = dual_scale[:, :, None, :]
    multipliers = basis_expand(coarse_solve(masked_loads, coarse_inverse), basis, inverse)
    residual = project(right_side - apply_dual(multipliers, schur, face_order, inverse), basis, face_order, inverse, coarse_inverse)
    search = project(scaling * residual, basis, face_order, inverse, coarse_inverse)
    direction = search
    for iteration in range(ITERS):
        dual_image = apply_dual(direction, schur, face_order, inverse)
        curvature = gram_product(direction, dual_image)
        descent = gram_product(direction, residual)
        projected_image = project(dual_image, basis, face_order, inverse, coarse_inverse)
        step_size = solve_small(curvature, descent)
        multipliers = multipliers + jnp.einsum('sjcm,cd->sjdm', direction, step_size, precision=highest)
        residual = residual - jnp.einsum('sjcm,cd->sjdm', projected_image, step_size, precision=highest)
        if iteration + 1 < ITERS:
            search = project(scaling * residual, basis, face_order, inverse, coarse_inverse)
            correction = -solve_small(curvature, gram_product(dual_image, search))
            direction = search + jnp.einsum('sjcm,cd->sjdm', direction, correction, precision=highest)
    return (multipliers, residual)
```

```python
import functools

import jax
import jax.numpy as jnp
from jax import lax
from jax.experimental import pallas as pl
from jax.experimental.pallas import tpu as pltpu
from jax.sharding import PartitionSpec as P

MESH = pl.DeviceIdType.MESH
CHAIN = 32
NSUB = 8
NZ = 8
NY = 4
CASES = 16
M = 384
MODES = 6
F32 = jnp.float32
BF16 = jnp.bfloat16
NN = (((1,), (0,)), ((), ()))
NT = (((1,), (1,)), ((), ()))


def parts(v):
    high = v.astype(BF16)
    return high, (v - high.astype(F32)).astype(BF16)


def mul(a, b, dims=NN):
    return lax.dot_general(a, b, dims, preferred_element_type=F32)


def mul3(a, b, dims=NN):
    ah, al = parts(a)
    bh, bl = parts(b)
    n = a.shape[0]
    both = mul(jnp.concatenate([ah, al], axis=0), bh, dims)
    return both[:n] + both[n:] + mul(ah, bl, dims)


def mulw(a, wh, wl):
    ah, al = parts(a)
    n = a.shape[0]
    both = mul(jnp.concatenate([ah, al], axis=0), wh)
    return both[:n] + both[n:] + mul(ah, wl)


def iota(shape, dim):
    return lax.broadcasted_iota(jnp.int32, shape, dim)


def fold_lanes(v):
    v = v + pltpu.roll(v, 64, 1)
    v = v + pltpu.roll(v, 32, 1)
    return v + pltpu.roll(v, 16, 1)


def inverse_of(matrix):
    lane = iota((CASES, 128), 1)
    row = iota((CASES, 128), 0)
    left = lane < CASES
    tile = jnp.where(left, matrix, jnp.where(lane == row + CASES, 1.0, 0.0))
    for k in range(CASES):
        column = jnp.broadcast_to(tile[:, k : k + 1], (CASES, 128))
        pivot_row = jnp.broadcast_to(tile[k : k + 1, :], (CASES, 128))
        pivot = jnp.broadcast_to(tile[k : k + 1, k : k + 1], (CASES, 128))
        scaled = pivot_row / pivot
        tile = jnp.where(row == k, scaled, tile - column * scaled)
    return tile[:, CASES : 2 * CASES]


def exact(a, b, dims=NN):
    return lax.dot_general(
        a, b, dims, precision=lax.Precision.HIGHEST, preferred_element_type=F32
    )


def kernel(
    right_ref, schur_hbm, modes_ref, count_ref, order_ref, scale_ref, loads_ref, coarse_ref,
    mult_ref, resid_ref,
    schur_ref, sh_ref, sl_ref, wh_ref, wl_ref, xa_ref,
    crow_ref, ch_ref, cl_ref,
    small1, small1_in, small2, small2_in,
    large1, large1_in, large2, large2_in,
    modes_out, modes_in,
    wide_fwd, wide_fwd_in, wide_back, wide_back_in,
    fwd, fwd_in, back, back_in,
    tmp_ref,
    load_sem, coarse_ssem, coarse_rsem, send1, recv1, send2, recv2, nb_ssem, nb_rsem,
):
    j = lax.axis_index("cluster")
    s = lax.axis_index("sub")
    y = j // NZ
    z = j % NZ
    me2 = y * NSUB + s

    load = pltpu.make_async_copy(schur_hbm, schur_ref, load_sem)
    load.start()

    def chain(d):
        return ((j + d + CHAIN) % CHAIN, s)

    def zpeer(i):
        return (y * NZ + (z + i) % NZ, s)

    def peer2(dy, ds):
        return (((y + dy) % NY) * NZ + z, (s + ds) % NSUB)

    def each_peer2(act):
        for dy in (2, 1, 3):
            def body(i, c, dy=dy):
                act(dy, i + 4)
                return c

            lax.fori_loop(0, NSUB, body, 0)
        for ds in (4, 3, 5, 2, 6, 1, 7):
            act(0, ds)

    def each_z(act):
        for i in (4, 3, 5, 2, 6, 1, 7):
            act(i)

    barrier = pltpu.get_barrier_semaphore()

    def greet(device):
        pl.semaphore_signal(barrier, inc=1, device_id=device, device_id_type=MESH)

    each_peer2(lambda dy, ds: greet(peer2(dy, ds)))
    each_z(lambda i: greet(zpeer(i)))
    for d in (-2, -1, 1, 2):
        greet(chain(d))

    count = count_ref[...]
    active = jnp.where(iota((MODES, 1), 0) < count, 1.0, 0.0)
    basis = modes_ref[...] * active
    lane = iota((8, 128), 1)
    sub8 = iota((8, 128), 0)
    tmp_ref[...] = jnp.zeros((8, 128), F32)
    tmp_ref[0:MODES, 0:CASES] = loads_ref[...] * active
    spread = fold_lanes(tmp_ref[...])
    own_loads = jnp.sum(jnp.where(lane // CASES == sub8, spread, 0.0), axis=0, keepdims=True)
    small1[0] = jnp.concatenate([own_loads, jnp.zeros((1, 128), F32)], axis=0)

    hot = jnp.where(iota((M, M), 0) == order_ref[...], 1.0, 0.0).astype(BF16)
    bh, bl = parts(basis[:, :M])
    third = (basis[:, :M] - bh.astype(F32) - bl.astype(F32)).astype(BF16)
    permuted = -(mul(bh, hot, NT) + mul(bl, hot, NT) + mul(third, hot, NT))
    modes_out[...] = jnp.zeros((8, M), F32)
    modes_out[0:MODES, :] = permuted

    pl.semaphore_wait(barrier, 31 + 7 + 4)

    def neighbour(k, src, dst, d):
        return pltpu.make_async_remote_copy(
            src_ref=src, dst_ref=dst, send_sem=nb_ssem.at[k], recv_sem=nb_rsem.at[k],
            device_id=chain(d), device_id_type=MESH,
        )

    def send_stage1(r, src, dst):
        def one(i):
            pltpu.make_async_remote_copy(
                src_ref=src, dst_ref=dst.at[z], send_sem=send1.at[r], recv_sem=recv1.at[r],
                device_id=zpeer(i), device_id_type=MESH,
            ).start()

        each_z(one)
        dst[z] = src[...]

    def wait_stage1(r, dst):
        w = dst.at[pl.ds(0, NZ - 1)]
        pltpu.make_async_copy(w, w, recv1.at[r]).wait()

    def send_stage2(r, src, dst):
        def one(dy, ds):
            pltpu.make_async_remote_copy(
                src_ref=src, dst_ref=dst.at[me2], send_sem=send2.at[r], recv_sem=recv2.at[r],
                device_id=peer2(dy, ds), device_id_type=MESH,
            ).start()

        each_peer2(one)
        dst[me2] = src[...]

    def wait_stage2(r, dst):
        w = dst.at[pl.ds(0, NY * NSUB - 1)]
        pltpu.make_async_copy(w, w, recv2.at[r]).wait()

    send_stage1(0, small1.at[0], small1_in.at[0])

    modes_copy = neighbour(0, modes_out, modes_in, -1)
    modes_copy.start()
    colour = j % 4
    coarse_copies = []
    for k, d in enumerate((1, -1, -2)):
        coarse_copies.append(
            pltpu.make_async_remote_copy(
                src_ref=coarse_ref, dst_ref=crow_ref.at[colour], send_sem=coarse_ssem.at[k],
                recv_sem=coarse_rsem.at[k], device_id=chain(d), device_id_type=MESH,
            )
        )
        coarse_copies[-1].start()
    crow_ref[colour] = coarse_ref[...]

    load.wait()

    def split_rows(i, c):
        rows = pl.ds(pl.multiple_of(i * 128, 128), 128)
        high, low = parts(schur_ref[rows, :])
        sh_ref[rows, :] = high
        sl_ref[rows, :] = low
        for ref, part in ((sh_ref, high), (sl_ref, low)):
            ref[rows, 0:M] = (-mul(part[:, :M], hot, NT)).astype(BF16)
        return c

    lax.fori_loop(0, 6, split_rows, 0)

    def split_columns(i, c):
        cols = pl.ds(pl.multiple_of(i * 128, 128), 128)
        for ref in (sh_ref, sl_ref):
            ref[0:M, cols] = (-mul(hot, ref[0:M, cols])).astype(BF16)
        return c

    lax.fori_loop(0, 6, split_columns, 0)

    first = j > 0
    last = j < CHAIN - 1

    def apply_send(k, rows, out, out_in):
        out[...] = rows
        copy = neighbour(k, out, out_in, 1)
        copy.start()
        return copy

    def apply_middle(copy, k, rows, out_in, ret, ret_in):
        copy.wait_recv()
        before = jnp.where(first, out_in[...], 0.0)
        image = mulw(jnp.concatenate([before, rows], axis=1), sh_ref[...], sl_ref[...])
        ret[...] = image[:, :M]
        copy_back = neighbour(k, ret, ret_in, -1)
        copy_back.start()
        return copy_back, image[:, M:]

    def apply_end(copy_back, own, ret_in):
        copy_back.wait_recv()
        return own + jnp.where(last, ret_in[...], 0.0)

    modes_copy.wait_recv()
    following = jnp.where(last, modes_in[...], 0.0)
    tmp_modes = jnp.concatenate([basis[:, M:], jnp.zeros((2, M), F32)], axis=0)
    xa_ref[:, 0:M] = jnp.zeros((32, M), F32)
    xa_ref[pl.ds(pl.multiple_of(colour * 8, 8), 8), 0:M] = tmp_modes
    xa_ref[pl.ds(pl.multiple_of(((j + 1) % 4) * 8, 8), 8), 0:M] = following
    expand = xa_ref[:, 0:M]
    wide_copy = apply_send(1, expand, wide_fwd, wide_fwd_in)

    pieces = []
    for block in (tmp_modes, following):
        for m in range(MODES):
            pieces.append(jnp.broadcast_to(block[m : m + 1, :], (CASES, M)))
        pieces.append(jnp.zeros((32, M), F32))
    weights = jnp.transpose(jnp.concatenate(pieces, axis=0))
    wh, wl = parts(weights)
    wh_ref[...] = wh
    wl_ref[...] = wl

    wide_back_copy, wide_own = apply_middle(wide_copy, 2, expand, wide_fwd_in, wide_back, wide_back_in)

    own_case = (iota((CASES, 256), 1) % CASES) == iota((CASES, 256), 0)
    below = sub8 > 0

    def coefficients(field):
        product = mulw(field, wh_ref[...], wl_ref[...])
        flat = jnp.sum(jnp.where(own_case, product, 0.0), axis=0, keepdims=True)
        return flat[:, :128], flat[:, 128:]

    def combine(own, nxt):
        moved = jnp.where(below, pltpu.roll(nxt, 1, 0), 0.0)
        end = jnp.broadcast_to(nxt[NZ - 1 : NZ, :], (8, 128))
        rest = jnp.where(
            sub8 == 0,
            pltpu.roll(end, 96, 1),
            jnp.where(sub8 == 1, pltpu.roll(end, 64, 1), pltpu.roll(end, 32, 1)),
        )
        return own + moved + jnp.where((lane >= 96) & (sub8 < 3), rest, 0.0)

    def stage2_small(r):
        wait_stage1(r, small1_in.at[r])
        got = small1_in[r]
        small2[r] = combine(got[:, 0, :], got[:, 1, :])
        send_stage2(r, small2.at[r], small2_in.at[r])

    slot = iota((8, 8, 128), 2) // CASES == iota((8, 8, 128), 0)

    def coarse(values):
        gh, gl = parts(values)
        both = mul(ch_ref[...], jnp.concatenate([gh, gl], axis=1))
        full = both[:, :128] + both[:, 128:] + mul(cl_ref[...], gh)
        picked = [
            jnp.sum(jnp.where(slot, full[c * 64 : (c + 1) * 64].reshape(8, 8, 128), 0.0), axis=0)
            for c in range(4)
        ]
        turned = jnp.transpose(jnp.concatenate(picked, axis=0))
        return jnp.sum(turned.reshape(8, CASES, 32), axis=0)

    def gram_rows(a, blocks):
        rep = jnp.concatenate([b for b in blocks for _ in range(8)], axis=0)
        product = mul3(a, rep, NT)
        rows = []
        for k in range(len(blocks)):
            tile = product[:, k * 128 : (k + 1) * 128].reshape(2, 8, 128)
            keep = iota((2, 8, 128), 2) // CASES == iota((2, 8, 128), 1)
            rows.append(jnp.sum(jnp.where(keep, tile, 0.0), axis=1))
        return rows

    def gram_matrix(pair):
        wide = jnp.broadcast_to(pair[:, None, :], (2, 8, 128))
        keep = iota((2, 8, 128), 2) // CASES == iota((2, 8, 128), 1)
        return fold_lanes(jnp.where(keep, wide, 0.0).reshape(CASES, 128))

    def send_large(r, own, nxt, rows):
        pad = jnp.zeros((8 - 2 - 2 * len(rows), 128), F32)
        large1[r] = jnp.concatenate([own, nxt, *rows, pad], axis=0)
        send_stage1(3 + r, large1.at[r], large1_in.at[r])

    def stage2_large(r):
        wait_stage1(3 + r, large1_in.at[r])
        got = large1_in[r]
        large2[r] = jnp.concatenate(
            [combine(got[:, 0, :], got[:, 1, :]), jnp.sum(got, axis=0)], axis=0
        )
        send_stage2(3 + r, large2.at[r], large2_in.at[r])

    def finish_large(r):
        wait_stage2(3 + r, large2_in.at[r])
        got = large2_in[r]
        sums = jnp.sum(got[:, 8:, :], axis=0)
        return got[:, :8, :].reshape(256, 128), sums

    def finish_small(r):
        wait_stage2(r, small2_in.at[r])
        return small2_in[r].reshape(256, 128)

    stage2_small(0)

    for copy in coarse_copies:
        copy.wait_recv()
    ch, cl = parts(crow_ref[...].reshape(256, 256))
    ch_ref[...] = ch
    cl_ref[...] = cl
    xa_ref[:, M:] = apply_end(wide_back_copy, wide_own, wide_back_in)

    right = right_ref[...]
    scale = scale_ref[...]
    y0 = coarse(finish_small(0))
    moved = mul3(y0, xa_ref[...])
    mult = moved[:, :M]
    tt = right - moved[:, M:]

    own, nxt = coefficients(tt)
    small1[1] = jnp.concatenate([own, nxt], axis=0)
    send_stage1(1, small1.at[1], small1_in.at[1])
    stage2_small(1)
    y1 = coarse(finish_small(1))
    resid = tt - mul3(y1, xa_ref[:, 0:M])
    scaled = scale * resid

    own, nxt = coefficients(scaled)
    small1[2] = jnp.concatenate([own, nxt], axis=0)
    send_stage1(2, small1.at[2], small1_in.at[2])
    copy = apply_send(3, scaled, fwd.at[0], fwd_in.at[0])
    copy_back, image_own = apply_middle(copy, 4, scaled, fwd_in.at[0], back.at[0], back_in.at[0])
    stage2_small(2)
    image = apply_end(copy_back, image_own, back_in.at[0])
    y2 = coarse(finish_small(2))
    moved = mul3(y2, xa_ref[...])
    direction = scaled - moved[:, :M]
    image = image - moved[:, M:]

    own, nxt = coefficients(image)
    send_large(0, own, nxt, gram_rows(direction, (image, resid)))
    stage2_large(0)
    values, sums = finish_large(0)
    y3 = coarse(values)
    projected = image - mul3(y3, xa_ref[:, 0:M])
    curvature_inverse = inverse_of(gram_matrix(sums[2:4]))
    descent = gram_matrix(sums[4:6])
    step = exact(curvature_inverse, descent)
    step_t = jnp.transpose(step)[0:CASES, :]
    mult = mult + exact(step_t, direction)
    resid = resid - exact(step_t, projected)
    scaled = scale * resid

    own, nxt = coefficients(scaled)
    send_large(1, own, nxt, gram_rows(projected, (scaled,)))
    copy = apply_send(5, scaled, fwd.at[1], fwd_in.at[1])
    copy_back, image_own = apply_middle(copy, 6, scaled, fwd_in.at[1], back.at[1], back_in.at[1])
    stage2_large(1)
    next_image = apply_end(copy_back, image_own, back_in.at[1])
    values, sums = finish_large(1)
    y4 = coarse(values)
    moved = mul3(y4, xa_ref[...])
    correction = -exact(curvature_inverse, gram_matrix(sums[2:4]))
    correction_t = jnp.transpose(correction)[0:CASES, :]
    mixed = exact(correction_t, jnp.concatenate([direction, image], axis=1))
    direction = scaled - moved[:, :M] + mixed[:, :M]
    image = next_image - moved[:, M:] + mixed[:, M:]

    own, nxt = coefficients(image)
    send_large(2, own, nxt, gram_rows(direction, (image, resid)))
    stage2_large(2)
    values, sums = finish_large(2)
    y5 = coarse(values)
    projected = image - mul3(y5, xa_ref[:, 0:M])
    step = exact(inverse_of(gram_matrix(sums[2:4])), gram_matrix(sums[4:6]))
    step_t = jnp.transpose(step)[0:CASES, :]
    mult_ref[...] = mult + exact(step_t, direction)
    resid_ref[...] = resid - exact(step_t, projected)

    modes_copy.wait_send()
    for c in coarse_copies:
        c.wait_send()
    for k, src, d in (
        (1, wide_fwd, 1), (2, wide_back, -1), (3, fwd.at[0], 1), (4, back.at[0], -1),
        (5, fwd.at[1], 1), (6, back.at[1], -1),
    ):
        pltpu.make_async_copy(src, src, nb_ssem.at[k]).wait()
    for r in range(6):
        in1 = small1_in.at[r] if r < 3 else large1_in.at[r - 3]
        in2 = small2_in.at[r] if r < 3 else large2_in.at[r - 3]
        w = in1.at[pl.ds(0, NZ - 1)]
        pltpu.make_async_copy(w, w, send1.at[r]).wait()
        w = in2.at[pl.ds(0, NY * NSUB - 1)]
        pltpu.make_async_copy(w, w, send2.at[r]).wait()


def coarse_blocks(rows):
    c = rows.reshape(MODES, NY, NZ, NSUB, MODES)
    main = jnp.transpose(c, (4, 0, 1, 3, 2))
    spare = c[:, 1:, 0].reshape(MODES, NY - 1, NSUB, 3, 2)
    spare = jnp.transpose(spare, (4, 0, 1, 2, 3))
    spare = jnp.pad(spare, ((0, 0), (0, 0), (0, 1), (0, 0), (0, NZ - 3)))
    both = jnp.concatenate([main, spare], axis=0)
    both = jnp.pad(both, ((0, 0), (0, 2), (0, 0), (0, 0), (0, 0)))
    return both.reshape(64, 256)


def shards(right, schur, modes, count, order, scale, loads, coarse):
    vmem = pl.BlockSpec(memory_space=pltpu.VMEM)
    dma = pltpu.SemaphoreType.DMA
    v = pltpu.VMEM
    mult, resid = pl.pallas_call(
        kernel,
        name="feti",
        out_shape=(jax.ShapeDtypeStruct((CASES, M), F32),) * 2,
        in_specs=[vmem, pl.BlockSpec(memory_space=pl.ANY)] + [vmem] * 6,
        out_specs=(vmem, vmem),
        scratch_shapes=[
            v((768, 768), F32), v((768, 768), BF16), v((768, 768), BF16),
            v((M, 256), BF16), v((M, 256), BF16), v((32, 768), F32),
            v((4, 64, 256), F32), v((256, 256), BF16), v((256, 256), BF16),
            v((3, 2, 128), F32), v((3, NZ, 2, 128), F32),
            v((3, 8, 128), F32), v((3, 32, 8, 128), F32),
            v((3, 8, 128), F32), v((3, NZ, 8, 128), F32),
            v((3, 16, 128), F32), v((3, 32, 16, 128), F32),
            v((8, M), F32), v((8, M), F32),
            v((32, M), F32), v((32, M), F32), v((32, M), F32), v((32, M), F32),
            v((2, 16, M), F32), v((2, 16, M), F32), v((2, 16, M), F32), v((2, 16, M), F32),
            v((8, 128), F32),
            dma, dma((3,)), dma((3,)), dma((6,)), dma((6,)), dma((6,)), dma((6,)),
            dma((7,)), dma((7,)),
        ],
        compiler_params=pltpu.CompilerParams(
            collective_id=0, has_side_effects=True, vmem_limit_bytes=40 * 1024 * 1024
        ),
    )(
        right.reshape(CASES, M), schur.reshape(768, 768), modes.reshape(MODES, 768), count,
        order.reshape(1, M), scale.reshape(1, M), loads.reshape(MODES, CASES),
        coarse_blocks(coarse),
    )
    return mult.reshape(1, 1, CASES, M), resid.reshape(1, 1, CASES, M)


def solution(mesh):
    field = P("sub", "cluster", None, None)
    return jax.shard_map(
        shards,
        mesh=mesh,
        in_specs=(
            field, field, field, P("sub", "cluster"), P("sub", "cluster", None),
            P("sub", "cluster", None), field, P(("cluster", "sub"), None),
        ),
        out_specs=(field, field),
        check_vma=False,
    )
```

```python
import functools

import jax
import jax.numpy as jnp
from jax import lax
from jax.experimental import pallas as pl
from jax.experimental.pallas import tpu as pltpu
from jax.sharding import PartitionSpec as P

MESH = pl.DeviceIdType.MESH
CHAIN = 32
NZ = 8
NY = 4
NX = 4
NC = 1536
CASES = 16
M = 384
MODES = 6
F32 = jnp.float32
BF16 = jnp.bfloat16
NN = (((1,), (0,)), ((), ()))
NT = (((1,), (1,)), ((), ()))
TN = (((0,), (0,)), ((), ()))


def parts(v):
    high = v.astype(BF16)
    return high, (v - high.astype(F32)).astype(BF16)


def mul(a, b, dims=NN):
    return lax.dot_general(a, b, dims, preferred_element_type=F32)


def mul3(a, b, dims=NN):
    ah, al = parts(a)
    bh, bl = parts(b)
    n = a.shape[0]
    both = mul(jnp.concatenate([ah, al], axis=0), bh, dims)
    return both[:n] + both[n:] + mul(ah, bl, dims)


def mulw(a, wh, wl):
    ah, al = parts(a)
    n = a.shape[0]
    both = mul(jnp.concatenate([ah, al], axis=0), wh)
    return both[:n] + both[n:] + mul(ah, wl)


def iota(shape, dim):
    return lax.broadcasted_iota(jnp.int32, shape, dim)


def fold_lanes(v):
    v = v + pltpu.roll(v, 64, 1)
    v = v + pltpu.roll(v, 32, 1)
    return v + pltpu.roll(v, 16, 1)


def eliminate(matrix, right):
    shape = (CASES, 2 * CASES)
    row = iota(shape, 0)
    tile = jnp.concatenate([matrix, right], axis=1)
    for k in range(0, CASES, 2):
        c1 = jnp.broadcast_to(tile[:, k : k + 1], shape)
        c2 = jnp.broadcast_to(tile[:, k + 1 : k + 2], shape)
        r1 = jnp.broadcast_to(tile[k : k + 1, :], shape)
        r2 = jnp.broadcast_to(tile[k + 1 : k + 2, :], shape)
        p11 = jnp.broadcast_to(c1[k : k + 1, :], shape)
        p21 = jnp.broadcast_to(c1[k + 1 : k + 2, :], shape)
        p12 = jnp.broadcast_to(c2[k : k + 1, :], shape)
        p22 = jnp.broadcast_to(c2[k + 1 : k + 2, :], shape)
        factor = p21 / p11
        s2 = (r2 - factor * r1) / (p22 - factor * p12)
        s1 = (r1 - p12 * s2) / p11
        rest = tile - c1 * s1 - c2 * s2
        tile = jnp.where(row == k, s1, jnp.where(row == k + 1, s2, rest))
    return tile[:, CASES:]


def exact(a, b, dims=NN):
    return lax.dot_general(
        a, b, dims, precision=lax.Precision.HIGHEST, preferred_element_type=F32
    )


FACES = (
    (2, 2), (2, 1), (2, 3), (1, 2), (3, 2), (2, 0), (0, 2), (1, 1), (1, 3), (3, 1), (3, 3),
    (0, 1), (0, 3), (1, 0), (3, 0), (0, 0),
)


def kernel(
    right_ref, schur_hbm, modes_ref, count_ref, order_ref, scale_ref, loads_ref, coarse_ref,
    mult_ref, resid_ref,
    schur_ref, sh_ref, sl_ref, wh_ref, wl_ref, xa_ref,
    cp_ref, crow_ref, ch_ref, cl_ref,
    out_ref, in_ref, pair_out, pair_in,
    gz_out, gz_in, gy_out, gy_in, gc_out, gc_in,
    left_out, left_in, right_out, right_in,
    fwd, fwd_in, wide_back, wide_back_in, back, back_in,
    tmp_ref,
    load_sem, plane_sem, all_sem, coarse_ssem, coarse_rsem, send, recv, pair_ssem, pair_rsem,
    gz_ssem, gz_rsem, gy_ssem, gy_rsem, gc_ssem, gc_rsem, nb_ssem, nb_rsem,
):
    j = lax.axis_index("cluster")
    s = lax.axis_index("sub")
    y = j // NZ
    z = j % NZ
    x = s // 2
    core = s % 2
    other = s + 1 - 2 * core
    place = j * NX + x
    face = y * NX + x

    load = pltpu.make_async_copy(schur_hbm, schur_ref, load_sem)
    load.start()

    def chain(d):
        return ((j + d + CHAIN) % CHAIN, s)

    def beside(d):
        return ((j + d + CHAIN) % CHAIN, other)

    def peer(dy, dx, dz):
        return (((y + dy) % NY) * NZ + (z + dz) % NZ, ((x + dx) % NX) * 2 + core)

    def z_offset(i):
        half = (i + 1) // 2
        return 4 + half * (1 - 2 * (i % 2))

    def run(faces, low, high, act):
        for dy, dx in faces:
            def body(i, c, dy=dy, dx=dx):
                act(dy, dx, z_offset(i))
                return c

            lax.fori_loop(low, high, body, 0)

    def far_peers(act):
        run(FACES[:11], 0, 5, act)
        run(FACES[:5], 5, 8, act)

    def near_peers(act):
        run(FACES[11:], 0, 5, act)
        run(FACES[5:15], 5, 8, act)
        run(FACES[15:], 5, 7, act)

    def every_peer(act):
        far_peers(act)
        near_peers(act)

    barrier = pltpu.get_barrier_semaphore()

    def greet(device):
        pl.semaphore_signal(barrier, inc=1, device_id=device, device_id_type=MESH)

    for dz in (4, 3, 5, 2, 6, 1, 7):
        greet(peer(0, 0, dz))
    for d in (-2, 2, -1, 1):
        greet(chain(d))
        greet(beside(d))
    for d in (2, 1, 3):
        greet(peer(d, 0, 0))
        greet(peer(0, d, 0))
    greet(beside(0))

    count = count_ref[...]
    active = jnp.where(iota((MODES, 1), 0) < count, 1.0, 0.0)
    basis = modes_ref[:, 0, :] * active
    sub8 = iota((8, 128), 0)
    tmp_ref[...] = jnp.zeros((8, 128), F32)
    tmp_ref[0:MODES, 0:CASES] = loads_ref[:, 0, :] * active
    spread = fold_lanes(tmp_ref[...])
    own_loads = jnp.sum(
        jnp.where(iota((8, 128), 1) // CASES == sub8, spread, 0.0), axis=0, keepdims=True
    )
    out_ref[0] = jnp.concatenate([own_loads, jnp.zeros((1, 128), F32)], axis=0)

    hot = jnp.where(iota((M, M), 0) == order_ref[...], 1.0, 0.0).astype(BF16)
    bh, bl = parts(basis[:, :M])
    permuted = -(mul(bh, hot, NT) + mul(bl, hot, NT))
    left_out[...] = jnp.concatenate([permuted, jnp.zeros((2, M), F32)], axis=0)
    right_out[...] = jnp.concatenate([basis[:, M:], jnp.zeros((2, M), F32)], axis=0)

    wanted = 12 * iota((NC, 128), 1)
    pick = jnp.where(iota((NC, 128), 0) == wanted, 1.0, 0.0).astype(BF16)
    rows = jnp.concatenate([coarse_ref[...], jnp.zeros((2, NC), F32)], axis=0)
    for c in range(2):
        shifted = []
        for m in range(MODES):
            d = c * MODES + m
            shifted.append(rows if d == 0 else pltpu.roll(rows, NC - d, 1))
        high, low = parts(jnp.concatenate(shifted, axis=0))
        cp_ref[c] = mul(high, pick) + mul(low, pick)

    pl.semaphore_wait(barrier, 22)

    def remote(src, dst, ssem, rsem, device):
        return pltpu.make_async_remote_copy(
            src_ref=src, dst_ref=dst, send_sem=ssem, recv_sem=rsem,
            device_id=device, device_id_type=MESH,
        )

    def neighbour(k, src, dst, d):
        return remote(src, dst, nb_ssem.at[k], nb_rsem.at[k], chain(d))

    left_copy = neighbour(0, left_out, left_in, -1)
    left_copy.start()
    right_copy = neighbour(1, right_out, right_in, 1)
    right_copy.start()
    colour = j % 4
    coarse_copies = []
    for k, d in enumerate((1, -1, -2)):
        coarse_copies.append(
            remote(cp_ref.at[core], crow_ref.at[0, colour], coarse_ssem.at[k], coarse_rsem.at[k], chain(d))
        )
    for k, d in enumerate((1, 0, -1, -2)):
        coarse_copies.append(
            remote(
                cp_ref.at[1 - core], crow_ref.at[1, colour], coarse_ssem.at[3 + k],
                coarse_rsem.at[3 + k], beside(d),
            )
        )

    for d in (2, 1, 3):
        pl.semaphore_signal(plane_sem, inc=1, device_id=peer(d, 0, 0), device_id_type=MESH)
    for copy in coarse_copies:
        copy.start()
    crow_ref[0, colour] = cp_ref[core]

    load.wait()

    def split_rows(i, c):
        rows = pl.ds(pl.multiple_of(i * 128, 128), 128)
        high, low = parts(schur_ref[rows, :])
        sh_ref[rows, :] = high
        sl_ref[rows, :] = low
        for ref, part in ((sh_ref, high), (sl_ref, low)):
            ref[rows, 0:M] = (-mul(part[:, :M], hot, NT)).astype(BF16)
        return c

    def split_columns(i, c):
        cols = pl.ds(pl.multiple_of(i * 128, 128), 128)
        for ref in (sh_ref, sl_ref):
            ref[0:M, cols] = (-mul(hot, ref[0:M, cols])).astype(BF16)
        return c

    lax.fori_loop(0, 6, split_rows, 0)
    pl.semaphore_wait(plane_sem, 3)
    for d in (2, 1, 3):
        pl.semaphore_signal(all_sem, inc=1, device_id=peer(0, d, 0), device_id_type=MESH)
    lax.fori_loop(0, 6, split_columns, 0)
    pl.semaphore_wait(all_sem, 3)

    def all_wait(ref, count, sem):
        w = ref.at[pl.ds(0, count)]
        pltpu.make_async_copy(w, w, sem).wait()

    landing = pl.ds(pl.multiple_of(2 * place, 2), 2)

    def start_send(r, dy, dx, dz):
        remote(out_ref.at[r], in_ref.at[r, landing], send.at[r], recv.at[r], peer(dy, dx, dz)).start()

    def send_own(r):
        in_ref[r, landing] = out_ref[r]

    def send_all(r):
        every_peer(functools.partial(start_send, r))
        send_own(r)

    send_all(0)

    first = j > 0
    last = j < CHAIN - 1

    def apply_product(before, own):
        lifted = jnp.concatenate([jnp.where(first, before, 0.0), own], axis=1)
        return mulw(lifted, sh_ref[...], sl_ref[...])

    def apply_send(i, values):
        fwd[i] = values
        copy = neighbour(3 + 2 * i, fwd.at[i], fwd_in.at[i], 1)
        copy.start()
        return copy

    def apply_middle(i, copy, values):
        copy.wait_recv()
        image = apply_product(fwd_in[i], values)
        back[i] = image[:, :M]
        copy_back = neighbour(4 + 2 * i, back.at[i], back_in.at[i], -1)
        copy_back.start()
        return copy_back, image[:, M:]

    def apply_end(i, copy_back, own):
        copy_back.wait_recv()
        return own + jnp.where(last, back_in[i], 0.0)

    left_copy.wait_recv()
    right_copy.wait_recv()
    following = jnp.where(last, left_in[...], 0.0)
    here = pl.ds(pl.multiple_of(colour * 8, 8), 8)
    after = pl.ds(pl.multiple_of(((j + 1) % 4) * 8, 8), 8)
    ahead = pl.ds(pl.multiple_of(((j + 3) % 4) * 8, 8), 8)
    xa_ref[...] = jnp.zeros((32, 768), F32)
    xa_ref[here, 0:M] = right_out[...]
    xa_ref[after, 0:M] = following
    xa_ref[here, M:] = left_out[...]
    xa_ref[ahead, M:] = right_in[...]
    wide_image = apply_product(xa_ref[:, M:], xa_ref[:, 0:M])
    wide_back[...] = wide_image[:, :M]
    wide_copy = neighbour(2, wide_back, wide_back_in, -1)
    wide_copy.start()
    xa_ref[:, M:] = wide_image[:, M:]

    pieces = []
    for block in (right_out[...], following):
        for m in range(MODES):
            pieces.append(jnp.broadcast_to(block[m : m + 1, :], (CASES, M)))
        pieces.append(jnp.zeros((32, M), F32))
    wh, wl = parts(jnp.transpose(jnp.concatenate(pieces, axis=0)))
    wh_ref[...] = wh
    wl_ref[...] = wl

    for copy in coarse_copies:
        copy.wait_recv()
    ch, cl = parts(crow_ref[...].reshape(384, 128))
    column = iota((128, 256), 1)
    spread = column // 2 + 4 * (column % 2)
    both = jnp.where(iota((128, 256), 0) == spread, 1.0, 0.0).astype(BF16)
    ch_ref[...] = mul(ch, both).astype(BF16)
    cl_ref[...] = mul(cl, both).astype(BF16)

    own_case = (iota((CASES, 256), 1) % CASES) == iota((CASES, 256), 0)
    slot = iota((MODES, 8, 128), 2) // CASES == iota((MODES, 8, 128), 0)

    def coefficients(r, field):
        product = mulw(field, wh_ref[...], wl_ref[...])
        flat = jnp.sum(jnp.where(own_case, product, 0.0), axis=0, keepdims=True)
        out_ref[r] = jnp.concatenate([flat[:, :128], flat[:, 128:]], axis=0)

    def picked(full, at):
        blocks = [
            jnp.sum(
                jnp.where(slot, full[at + c * 48 : at + (c + 1) * 48].reshape(MODES, 8, 128), 0.0),
                axis=0,
            )
            for c in range(4)
        ]
        return jnp.concatenate(blocks, axis=0)

    def coarse(r):
        all_wait(in_ref.at[r], 254, recv.at[r])
        gh, gl = parts(in_ref[r])
        both = mul(ch_ref[...], jnp.concatenate([gh, gl], axis=1))
        full = both[:, :128] + both[:, 128:] + mul(cl_ref[...], gh)
        pair_out[r] = picked(full, 192)
        copy = remote(pair_out.at[r], pair_in.at[r], pair_ssem.at[r], pair_rsem.at[r], beside(0))
        copy.start()
        mine = picked(full, 0)
        copy.wait_recv()
        turned = jnp.transpose(mine + pair_in[r])
        return jnp.sum(turned.reshape(8, CASES, 32), axis=0)

    def grams(a, blocks):
        spare = jnp.zeros((128 - CASES * len(blocks), M), F32)
        return mul3(a, jnp.concatenate([*blocks, spare], axis=0), NT)

    def gram_z(i, values):
        gz_out[i] = values
        for dz in (4, 3, 5, 2, 6, 1, 7):
            remote(gz_out.at[i], gz_in.at[i, z], gz_ssem.at[i], gz_rsem.at[i], peer(0, 0, dz)).start()
        gz_in[i, z] = values

    def gram_y(i):
        all_wait(gz_in.at[i], NZ - 1, gz_rsem.at[i])
        values = jnp.sum(gz_in[i], axis=0)
        gy_out[i] = values
        for dy, dx in FACES[:15]:
            remote(
                gy_out.at[i], gy_in.at[i, face], gy_ssem.at[i], gy_rsem.at[i], peer(dy, dx, 0)
            ).start()
        gy_in[i, face] = values

    def gram_pair(i):
        all_wait(gy_in.at[i], NY * NX - 1, gy_rsem.at[i])
        values = jnp.sum(gy_in[i], axis=0)
        gc_out[i] = values
        copy = remote(gc_out.at[i], gc_in.at[i], gc_ssem.at[i], gc_rsem.at[i], beside(0))
        copy.start()
        return copy, values

    def gram_end(i, copy, values):
        copy.wait_recv()
        return values + gc_in[i]

    right = right_ref[...]
    scale = scale_ref[...]
    y0 = coarse(0)
    wide_copy.wait_recv()
    xa_ref[:, M:] = xa_ref[:, M:] + jnp.where(last, wide_back_in[...], 0.0)
    moved = mul3(y0, xa_ref[...])
    mult = moved[:, :M]
    tt = right - moved[:, M:]

    coefficients(1, tt)
    send_all(1)
    resid = tt - mul3(coarse(1), xa_ref[:, 0:M])
    scaled = scale * resid

    coefficients(2, scaled)
    copy = apply_send(0, scaled)
    send_all(2)
    copy_back, own = apply_middle(0, copy, scaled)
    y2 = coarse(2)
    p = apply_end(0, copy_back, own)
    moved = mul3(y2, xa_ref[...])
    a = scaled - moved[:, :M]
    p = p - moved[:, M:]

    coefficients(3, p)
    send_all(3)
    gram_z(0, grams(a, (p, resid)))
    q = p - mul3(coarse(3), xa_ref[:, 0:M])
    scaled = scale * q

    coefficients(4, scaled)
    copy = apply_send(1, scaled)
    send_all(4)
    copy_back, own = apply_middle(1, copy, scaled)
    gram_y(0)
    crossed = grams(a, (q,))
    y4 = coarse(4)
    u = apply_end(1, copy_back, own)
    moved = mul3(y4, xa_ref[...])
    w = scaled - moved[:, :M]
    u = u - moved[:, M:]

    coefficients(5, u)
    lane = iota((CASES, 128), 1)
    gram_z(1, grams(w, (p, u, resid, q)) + jnp.where(lane >= 64, pltpu.roll(crossed, 64, 1), 0.0))
    far_peers(functools.partial(start_send, 5))
    copy, values = gram_pair(0)
    near_peers(functools.partial(start_send, 5))
    send_own(5)
    gram_y(1)
    sums = gram_end(0, copy, values)
    ap, ar = (sums[:, k * CASES : (k + 1) * CASES] for k in range(2))
    eye = jnp.where(iota((CASES, CASES), 0) == iota((CASES, CASES), 1), 1.0, 0.0)
    inverse = eliminate(ap, eye)
    alpha = exact(inverse, ar)
    v = u - mul3(coarse(5), xa_ref[:, 0:M])
    copy, values = gram_pair(1)
    sums = gram_end(1, copy, values)
    wp, wu, wr, wq, aq = (sums[:, k * CASES : (k + 1) * CASES] for k in range(5))
    across = exact(inverse, wp, NT)
    stepped = exact(jnp.concatenate([wq, aq], axis=0), alpha)
    rest = ar - stepped[CASES:]
    reduced = exact(across, rest, TN)
    gamma = eliminate(wu - exact(wp, across), wr - stepped[:CASES] - reduced)
    delta = alpha - exact(across, gamma)
    mix = jnp.transpose(jnp.concatenate([delta, gamma], axis=1))
    mixed = exact(mix[:CASES], jnp.concatenate([a, q], axis=1)) + exact(
        mix[CASES:], jnp.concatenate([w, v], axis=1)
    )
    mult_ref[...] = mult + mixed[:, :M]
    resid_ref[...] = resid - mixed[:, M:]

    left_copy.wait_send()
    right_copy.wait_send()
    for copy in coarse_copies:
        copy.wait_send()
    pltpu.make_async_copy(wide_back, wide_back, nb_ssem.at[2]).wait()
    for i in range(2):
        pltpu.make_async_copy(fwd.at[i], fwd.at[i], nb_ssem.at[3 + 2 * i]).wait()
        pltpu.make_async_copy(back.at[i], back.at[i], nb_ssem.at[4 + 2 * i]).wait()
        all_wait(gz_in.at[i], NZ - 1, gz_ssem.at[i])
        all_wait(gy_in.at[i], NY * NX - 1, gy_ssem.at[i])
        pltpu.make_async_copy(gc_out.at[i], gc_out.at[i], gc_ssem.at[i]).wait()
    for r in range(6):
        all_wait(in_ref.at[r], 254, send.at[r])
        pltpu.make_async_copy(pair_out.at[r], pair_out.at[r], pair_ssem.at[r]).wait()


def shards(right, schur, modes, count, order, scale, loads, coarse):
    vmem = pl.BlockSpec(memory_space=pltpu.VMEM)
    dma = pltpu.SemaphoreType.DMA
    regular = pltpu.SemaphoreType.REGULAR
    v = pltpu.VMEM
    mult, resid = pl.pallas_call(
        kernel,
        name="feti",
        out_shape=(jax.ShapeDtypeStruct((CASES, M), F32),) * 2,
        in_specs=[vmem, pl.BlockSpec(memory_space=pltpu.HBM)] + [vmem] * 6,
        out_specs=(vmem, vmem),
        scratch_shapes=[
            v((768, 768), F32), v((768, 768), BF16), v((768, 768), BF16),
            v((M, 256), BF16), v((M, 256), BF16), v((32, 768), F32),
            v((2, 48, 128), F32), v((2, 4, 48, 128), F32), v((384, 256), BF16), v((384, 256), BF16),
            v((6, 2, 128), F32), v((6, 256, 128), F32), v((6, 32, 128), F32), v((6, 32, 128), F32),
            v((2, 16, 128), F32), v((2, NZ, 16, 128), F32),
            v((2, 16, 128), F32), v((2, NY * NX, 16, 128), F32),
            v((2, 16, 128), F32), v((2, 16, 128), F32),
            v((8, M), F32), v((8, M), F32), v((8, M), F32), v((8, M), F32),
            v((2, 16, M), F32), v((2, 16, M), F32), v((32, M), F32), v((32, M), F32),
            v((2, 16, M), F32), v((2, 16, M), F32),
            v((8, 128), F32),
            dma, regular, regular, dma((7,)), dma((7,)), dma((6,)), dma((6,)), dma((6,)), dma((6,)),
            dma((2,)), dma((2,)), dma((2,)), dma((2,)), dma((2,)), dma((2,)), dma((7,)), dma((7,)),
        ],
        compiler_params=pltpu.CompilerParams(
            collective_id=0, has_side_effects=True, vmem_limit_bytes=60 * 1024 * 1024
        ),
    )(
        right.reshape(CASES, M), schur.reshape(768, 768), modes.reshape(MODES, 1, 768), count,
        order.reshape(1, M), scale.reshape(1, M), loads.reshape(MODES, 1, CASES), coarse,
    )
    return mult.reshape(1, 1, CASES, M), resid.reshape(1, 1, CASES, M)


def solution(mesh):
    field = P("sub", "cluster", None, None)
    return jax.shard_map(
        shards,
        mesh=mesh,
        in_specs=(
            field, field, field, P("sub", "cluster"), P("sub", "cluster", None),
            P("sub", "cluster", None), field, P(("cluster", "sub"), None),
        ),
        out_specs=(field, field),
        check_vma=False,
    )
```

```python
import functools

import jax
import jax.numpy as jnp
from jax import lax
from jax.experimental import pallas as pl
from jax.experimental.pallas import tpu as pltpu
from jax.sharding import PartitionSpec as P

MESH = pl.DeviceIdType.MESH
CHAIN = 32
NZ = 8
NY = 4
NX = 4
NC = 1536
CASES = 16
M = 384
MODES = 6
F32 = jnp.float32
BF16 = jnp.bfloat16
NN = (((1,), (0,)), ((), ()))
NT = (((1,), (1,)), ((), ()))
TN = (((0,), (0,)), ((), ()))


def parts(v):
    high = v.astype(BF16)
    return high, (v - high.astype(F32)).astype(BF16)


def mul(a, b, dims=NN):
    return lax.dot_general(a, b, dims, preferred_element_type=F32)


def mul3(a, b, dims=NN):
    ah, al = parts(a)
    bh, bl = parts(b)
    n = a.shape[0]
    both = mul(jnp.concatenate([ah, al], axis=0), bh, dims)
    return both[:n] + both[n:] + mul(ah, bl, dims)


def mulw(a, wh, wl):
    ah, al = parts(a)
    n = a.shape[0]
    both = mul(jnp.concatenate([ah, al], axis=0), wh)
    return both[:n] + both[n:] + mul(ah, wl)


def iota(shape, dim):
    return lax.broadcasted_iota(jnp.int32, shape, dim)


def fold_lanes(v):
    v = v + pltpu.roll(v, 64, 1)
    v = v + pltpu.roll(v, 32, 1)
    return v + pltpu.roll(v, 16, 1)


def eliminate(matrix, right):
    shape = (CASES, 2 * CASES)
    row = iota(shape, 0)
    tile = jnp.concatenate([matrix, right], axis=1)
    for k in range(0, CASES, 2):
        c1 = jnp.broadcast_to(tile[:, k : k + 1], shape)
        c2 = jnp.broadcast_to(tile[:, k + 1 : k + 2], shape)
        r1 = jnp.broadcast_to(tile[k : k + 1, :], shape)
        r2 = jnp.broadcast_to(tile[k + 1 : k + 2, :], shape)
        p11 = jnp.broadcast_to(c1[k : k + 1, :], shape)
        p21 = jnp.broadcast_to(c1[k + 1 : k + 2, :], shape)
        p12 = jnp.broadcast_to(c2[k : k + 1, :], shape)
        p22 = jnp.broadcast_to(c2[k + 1 : k + 2, :], shape)
        factor = p21 / p11
        s2 = (r2 - factor * r1) / (p22 - factor * p12)
        s1 = (r1 - p12 * s2) / p11
        rest = tile - c1 * s1 - c2 * s2
        tile = jnp.where(row == k, s1, jnp.where(row == k + 1, s2, rest))
    return tile[:, CASES:]


def exact(a, b, dims=NN):
    return lax.dot_general(
        a, b, dims, precision=lax.Precision.HIGHEST, preferred_element_type=F32
    )


def ring(distance, size):
    return min(distance, size - distance)


OFFSETS = sorted(
    (
        (dy, dx, dz)
        for dy in (2, 1, 3, 0)
        for dx in (2, 1, 3, 0)
        for dz in (4, 3, 5, 2, 6, 1, 7, 0)
        if dy or dx or dz
    ),
    key=lambda o: -(ring(o[0], NY) + ring(o[1], NX) + ring(o[2], NZ)),
)


def kernel(
    right_hbm, schur_hbm, modes_hbm, count_hbm, order_hbm, scale_hbm, loads_hbm, coarse_hbm,
    mult_ref, resid_ref,
    right_ref, modes_ref, count_ref, order_ref, scale_ref, loads_ref, coarse_ref,
    schur_ref, sh_ref, sl_ref, wh_ref, wl_ref, xa_ref,
    cp_ref, crow_ref, ch_ref, cl_ref,
    out_ref, in_ref, pair_out, pair_in,
    gz_out, gz_in, gy_out, gy_in, gc_out, gc_in,
    left_out, left_in, right_out, right_in,
    fwd, fwd_in, wide_back, wide_back_in, back, back_in,
    tmp_ref,
    load_sem, plane_sem, all_sem, coarse_ssem, coarse_rsem, send, recv, pair_ssem, pair_rsem,
    gz_ssem, gz_rsem, gy_ssem, gy_rsem, gc_ssem, gc_rsem, nb_ssem, nb_rsem,
):
    j = lax.axis_index("cluster")
    s = lax.axis_index("sub")
    y = j // NZ
    z = j % NZ
    x = s // 2
    core = s % 2
    other = s + 1 - 2 * core
    place = j * NX + x
    face = y * NX + x

    def chain(d):
        return ((j + d + CHAIN) % CHAIN, s)

    def beside(d):
        return ((j + d + CHAIN) % CHAIN, other)

    ys = [((y + d) % NY) * NZ for d in range(NY)]
    zs = [(z + d) % NZ for d in range(NZ)]
    xs = [((x + d) % NX) * 2 + core for d in range(NX)]

    def peer(dy, dx, dz):
        return (ys[dy] + zs[dz], xs[dx])

    barrier = pltpu.get_barrier_semaphore()

    def greet(device):
        pl.semaphore_signal(barrier, inc=1, device_id=device, device_id_type=MESH)

    for dz in (4, 3, 5, 2, 6, 1, 7):
        greet(peer(0, 0, dz))
    for d in (-2, 2, -1, 1):
        greet(chain(d))
        greet(beside(d))
    for d in (2, 1, 3):
        greet(peer(d, 0, 0))
        greet(peer(0, d, 0))
    greet(beside(0))

    loads = [
        pltpu.make_async_copy(src, dst, load_sem.at[k])
        for k, (src, dst) in enumerate(
            (
                (loads_hbm, loads_ref), (count_hbm, count_ref), (modes_hbm, modes_ref),
                (order_hbm, order_ref), (coarse_hbm, coarse_ref), (schur_hbm, schur_ref),
                (right_hbm, right_ref), (scale_hbm, scale_ref),
            )
        )
    ]
    for copy in loads:
        copy.start()
    for copy in loads[:4]:
        copy.wait()

    count = count_ref[...]
    active = jnp.where(iota((MODES, 1), 0) < count, 1.0, 0.0)
    basis = modes_ref[:, 0, :] * active
    sub8 = iota((8, 128), 0)
    tmp_ref[...] = jnp.zeros((8, 128), F32)
    tmp_ref[0:MODES, 0:CASES] = loads_ref[:, 0, :] * active
    spread = fold_lanes(tmp_ref[...])
    own_loads = jnp.sum(
        jnp.where(iota((8, 128), 1) // CASES == sub8, spread, 0.0), axis=0, keepdims=True
    )
    out_ref[0] = jnp.concatenate([own_loads, jnp.zeros((1, 128), F32)], axis=0)

    hot = jnp.where(iota((M, M), 0) == order_ref[...], 1.0, 0.0).astype(BF16)
    bh, bl = parts(basis[:, :M])
    permuted = -(mul(bh, hot, NT) + mul(bl, hot, NT))
    left_out[...] = jnp.concatenate([permuted, jnp.zeros((2, M), F32)], axis=0)
    right_out[...] = jnp.concatenate([basis[:, M:], jnp.zeros((2, M), F32)], axis=0)

    loads[4].wait()
    wanted = 12 * iota((NC, 128), 1)
    pick = jnp.where(iota((NC, 128), 0) == wanted, 1.0, 0.0).astype(BF16)
    rows = jnp.concatenate([coarse_ref[...], jnp.zeros((2, NC), F32)], axis=0)
    for c in range(2):
        shifted = []
        for m in range(MODES):
            d = c * MODES + m
            shifted.append(rows if d == 0 else pltpu.roll(rows, NC - d, 1))
        high, low = parts(jnp.concatenate(shifted, axis=0))
        cp_ref[c] = mul(high, pick) + mul(low, pick)

    pl.semaphore_wait(barrier, 22)

    def remote(src, dst, ssem, rsem, device):
        return pltpu.make_async_remote_copy(
            src_ref=src, dst_ref=dst, send_sem=ssem, recv_sem=rsem,
            device_id=device, device_id_type=MESH,
        )

    def neighbour(k, src, dst, d):
        return remote(src, dst, nb_ssem.at[k], nb_rsem.at[k], chain(d))

    left_copy = neighbour(0, left_out, left_in, -1)
    left_copy.start()
    right_copy = neighbour(1, right_out, right_in, 1)
    right_copy.start()
    colour = j % 4
    coarse_copies = []
    for k, d in enumerate((1, -1, -2)):
        coarse_copies.append(
            remote(cp_ref.at[core], crow_ref.at[0, colour], coarse_ssem.at[k], coarse_rsem.at[k], chain(d))
        )
    for k, d in enumerate((1, 0, -1, -2)):
        coarse_copies.append(
            remote(
                cp_ref.at[1 - core], crow_ref.at[1, colour], coarse_ssem.at[3 + k],
                coarse_rsem.at[3 + k], beside(d),
            )
        )

    for d in (2, 1, 3):
        pl.semaphore_signal(plane_sem, inc=1, device_id=peer(d, 0, 0), device_id_type=MESH)
    for copy in coarse_copies:
        copy.start()
    crow_ref[0, colour] = cp_ref[core]

    for copy in loads[5:]:
        copy.wait()

    def split_rows(i, c):
        rows = pl.ds(pl.multiple_of(i * 128, 128), 128)
        high, low = parts(schur_ref[rows, :])
        sh_ref[rows, :] = high
        sl_ref[rows, :] = low
        for ref, part in ((sh_ref, high), (sl_ref, low)):
            ref[rows, 0:M] = (-mul(part[:, :M], hot, NT)).astype(BF16)
        return c

    def split_columns(i, c):
        cols = pl.ds(pl.multiple_of(i * 128, 128), 128)
        for ref in (sh_ref, sl_ref):
            ref[0:M, cols] = (-mul(hot, ref[0:M, cols])).astype(BF16)
        return c

    lax.fori_loop(0, 6, split_rows, 0)
    pl.semaphore_wait(plane_sem, 3)
    for d in (2, 1, 3):
        pl.semaphore_signal(all_sem, inc=1, device_id=peer(0, d, 0), device_id_type=MESH)
    lax.fori_loop(0, 6, split_columns, 0)
    pl.semaphore_wait(all_sem, 3)

    def all_wait(ref, count, sem):
        w = ref.at[pl.ds(0, count)]
        pltpu.make_async_copy(w, w, sem).wait()

    landing = pl.ds(pl.multiple_of(2 * place, 2), 2)

    def start_send(r, dy, dx, dz):
        remote(out_ref.at[r], in_ref.at[r, landing], send.at[r], recv.at[r], peer(dy, dx, dz)).start()

    def send_own(r):
        in_ref[r, landing] = out_ref[r]

    def send_some(r, offsets):
        for offset in offsets:
            start_send(r, *offset)

    def send_all(r):
        send_some(r, OFFSETS)
        send_own(r)

    send_all(0)

    first = j > 0
    last = j < CHAIN - 1

    def apply_product(before, own):
        lifted = jnp.concatenate([jnp.where(first, before, 0.0), own], axis=1)
        return mulw(lifted, sh_ref[...], sl_ref[...])

    def apply_send(i, values):
        fwd[i] = values
        copy = neighbour(3 + 2 * i, fwd.at[i], fwd_in.at[i], 1)
        copy.start()
        return copy

    def apply_middle(i, copy, values):
        copy.wait_recv()
        image = apply_product(fwd_in[i], values)
        back[i] = image[:, :M]
        copy_back = neighbour(4 + 2 * i, back.at[i], back_in.at[i], -1)
        copy_back.start()
        return copy_back, image[:, M:]

    def apply_end(i, copy_back, own):
        copy_back.wait_recv()
        return own + jnp.where(last, back_in[i], 0.0)

    left_copy.wait_recv()
    right_copy.wait_recv()
    following = jnp.where(last, left_in[...], 0.0)
    here = pl.ds(pl.multiple_of(colour * 8, 8), 8)
    after = pl.ds(pl.multiple_of(((j + 1) % 4) * 8, 8), 8)
    ahead = pl.ds(pl.multiple_of(((j + 3) % 4) * 8, 8), 8)
    xa_ref[...] = jnp.zeros((32, 768), F32)
    xa_ref[here, 0:M] = right_out[...]
    xa_ref[after, 0:M] = following
    xa_ref[here, M:] = left_out[...]
    xa_ref[ahead, M:] = right_in[...]
    wide_image = apply_product(xa_ref[:, M:], xa_ref[:, 0:M])
    wide_back[...] = wide_image[:, :M]
    wide_copy = neighbour(2, wide_back, wide_back_in, -1)
    wide_copy.start()
    xa_ref[:, M:] = wide_image[:, M:]

    pieces = []
    for block in (right_out[...], following):
        for m in range(MODES):
            pieces.append(jnp.broadcast_to(block[m : m + 1, :], (CASES, M)))
        pieces.append(jnp.zeros((32, M), F32))
    wh, wl = parts(jnp.transpose(jnp.concatenate(pieces, axis=0)))
    wh_ref[...] = wh
    wl_ref[...] = wl

    for copy in coarse_copies:
        copy.wait_recv()
    ch, cl = parts(crow_ref[...].reshape(384, 128))
    column = iota((128, 256), 1)
    spread = column // 2 + 4 * (column % 2)
    both = jnp.where(iota((128, 256), 0) == spread, 1.0, 0.0).astype(BF16)
    ch_ref[...] = mul(ch, both).astype(BF16)
    cl_ref[...] = mul(cl, both).astype(BF16)

    own_case = (iota((CASES, 256), 1) % CASES) == iota((CASES, 256), 0)
    slot = iota((MODES, 8, 128), 2) // CASES == iota((MODES, 8, 128), 0)

    def coefficients(r, field):
        product = mulw(field, wh_ref[...], wl_ref[...])
        flat = jnp.sum(jnp.where(own_case, product, 0.0), axis=0, keepdims=True)
        out_ref[r] = jnp.concatenate([flat[:, :128], flat[:, 128:]], axis=0)

    def picked(full, at):
        blocks = [
            jnp.sum(
                jnp.where(slot, full[at + c * 48 : at + (c + 1) * 48].reshape(MODES, 8, 128), 0.0),
                axis=0,
            )
            for c in range(4)
        ]
        return jnp.concatenate(blocks, axis=0)

    def coarse(r):
        all_wait(in_ref.at[r], 254, recv.at[r])
        gh, gl = parts(in_ref[r])
        both = mul(ch_ref[...], jnp.concatenate([gh, gl], axis=1))
        full = both[:, :128] + both[:, 128:] + mul(cl_ref[...], gh)
        pair_out[r] = picked(full, 192)
        copy = remote(pair_out.at[r], pair_in.at[r], pair_ssem.at[r], pair_rsem.at[r], beside(0))
        copy.start()
        mine = picked(full, 0)
        copy.wait_recv()
        turned = jnp.transpose(mine + pair_in[r])
        return jnp.sum(turned.reshape(8, CASES, 32), axis=0)

    def grams(a, blocks):
        spare = jnp.zeros((128 - CASES * len(blocks), M), F32)
        return mul3(a, jnp.concatenate([*blocks, spare], axis=0), NT)

    def gram_z(i, values):
        gz_out[i] = values
        for dz in (4, 3, 5, 2, 6, 1, 7):
            remote(gz_out.at[i], gz_in.at[i, z], gz_ssem.at[i], gz_rsem.at[i], peer(0, 0, dz)).start()
        gz_in[i, z] = values

    def gram_y(i):
        all_wait(gz_in.at[i], NZ - 1, gz_rsem.at[i])
        values = jnp.sum(gz_in[i], axis=0)
        gy_out[i] = values
        for dy, dx, dz in OFFSETS:
            if dz:
                continue
            remote(
                gy_out.at[i], gy_in.at[i, face], gy_ssem.at[i], gy_rsem.at[i], peer(dy, dx, 0)
            ).start()
        gy_in[i, face] = values

    def gram_pair(i):
        all_wait(gy_in.at[i], NY * NX - 1, gy_rsem.at[i])
        values = jnp.sum(gy_in[i], axis=0)
        gc_out[i] = values
        copy = remote(gc_out.at[i], gc_in.at[i], gc_ssem.at[i], gc_rsem.at[i], beside(0))
        copy.start()
        return copy, values

    def gram_end(i, copy, values):
        copy.wait_recv()
        return values + gc_in[i]

    right = right_ref[...]
    scale = scale_ref[...]
    y0 = coarse(0)
    wide_copy.wait_recv()
    xa_ref[:, M:] = xa_ref[:, M:] + jnp.where(last, wide_back_in[...], 0.0)
    moved = mul3(y0, xa_ref[...])
    mult = moved[:, :M]
    tt = right - moved[:, M:]

    coefficients(1, tt)
    send_all(1)
    resid = tt - mul3(coarse(1), xa_ref[:, 0:M])
    scaled = scale * resid

    coefficients(2, scaled)
    copy = apply_send(0, scaled)
    send_all(2)
    copy_back, own = apply_middle(0, copy, scaled)
    y2 = coarse(2)
    p = apply_end(0, copy_back, own)
    moved = mul3(y2, xa_ref[...])
    a = scaled - moved[:, :M]
    p = p - moved[:, M:]

    coefficients(3, p)
    send_all(3)
    gram_z(0, grams(a, (p, resid)))
    q = p - mul3(coarse(3), xa_ref[:, 0:M])
    scaled = scale * q

    coefficients(4, scaled)
    copy = apply_send(1, scaled)
    send_all(4)
    copy_back, own = apply_middle(1, copy, scaled)
    gram_y(0)
    crossed = grams(a, (q,))
    y4 = coarse(4)
    u = apply_end(1, copy_back, own)
    moved = mul3(y4, xa_ref[...])
    w = scaled - moved[:, :M]
    u = u - moved[:, M:]

    coefficients(5, u)
    lane = iota((CASES, 128), 1)
    gram_z(1, grams(w, (p, u, resid, q)) + jnp.where(lane >= 64, pltpu.roll(crossed, 64, 1), 0.0))
    send_some(5, OFFSETS[:64])
    copy, values = gram_pair(0)
    send_some(5, OFFSETS[64:])
    send_own(5)
    gram_y(1)
    sums = gram_end(0, copy, values)
    ap, ar = (sums[:, k * CASES : (k + 1) * CASES] for k in range(2))
    eye = jnp.where(iota((CASES, CASES), 0) == iota((CASES, CASES), 1), 1.0, 0.0)
    inverse = eliminate(ap, eye)
    alpha = exact(inverse, ar)
    v = u - mul3(coarse(5), xa_ref[:, 0:M])
    copy, values = gram_pair(1)
    sums = gram_end(1, copy, values)
    wp, wu, wr, wq, aq = (sums[:, k * CASES : (k + 1) * CASES] for k in range(5))
    across = exact(inverse, wp, NT)
    stepped = exact(jnp.concatenate([wq, aq], axis=0), alpha)
    rest = ar - stepped[CASES:]
    reduced = exact(across, rest, TN)
    gamma = eliminate(wu - exact(wp, across), wr - stepped[:CASES] - reduced)
    delta = alpha - exact(across, gamma)
    mix = jnp.transpose(jnp.concatenate([delta, gamma], axis=1))
    mixed = exact(mix[:CASES], jnp.concatenate([a, q], axis=1)) + exact(
        mix[CASES:], jnp.concatenate([w, v], axis=1)
    )
    mult_ref[...] = mult + mixed[:, :M]
    resid_ref[...] = resid - mixed[:, M:]

    left_copy.wait_send()
    right_copy.wait_send()
    for copy in coarse_copies:
        copy.wait_send()
    pltpu.make_async_copy(wide_back, wide_back, nb_ssem.at[2]).wait()
    for i in range(2):
        pltpu.make_async_copy(fwd.at[i], fwd.at[i], nb_ssem.at[3 + 2 * i]).wait()
        pltpu.make_async_copy(back.at[i], back.at[i], nb_ssem.at[4 + 2 * i]).wait()
        all_wait(gz_in.at[i], NZ - 1, gz_ssem.at[i])
        all_wait(gy_in.at[i], NY * NX - 1, gy_ssem.at[i])
        pltpu.make_async_copy(gc_out.at[i], gc_out.at[i], gc_ssem.at[i]).wait()
    for r in range(6):
        all_wait(in_ref.at[r], 254, send.at[r])
        pltpu.make_async_copy(pair_out.at[r], pair_out.at[r], pair_ssem.at[r]).wait()


def shards(right, schur, modes, count, order, scale, loads, coarse):
    vmem = pl.BlockSpec(memory_space=pltpu.VMEM)
    dma = pltpu.SemaphoreType.DMA
    regular = pltpu.SemaphoreType.REGULAR
    v = pltpu.VMEM
    mult, resid = pl.pallas_call(
        kernel,
        name="feti",
        out_shape=(jax.ShapeDtypeStruct((CASES, M), F32),) * 2,
        in_specs=[pl.BlockSpec(memory_space=pltpu.HBM)] * 8,
        out_specs=(vmem, vmem),
        scratch_shapes=[
            v((CASES, M), F32), v((MODES, 1, 768), F32), v((1, 1), jnp.int32), v((1, M), jnp.int32),
            v((1, M), F32), v((MODES, 1, CASES), F32), v((MODES, NC), F32),
            v((768, 768), F32), v((768, 768), BF16), v((768, 768), BF16),
            v((M, 256), BF16), v((M, 256), BF16), v((32, 768), F32),
            v((2, 48, 128), F32), v((2, 4, 48, 128), F32), v((384, 256), BF16), v((384, 256), BF16),
            v((6, 2, 128), F32), v((6, 256, 128), F32), v((6, 32, 128), F32), v((6, 32, 128), F32),
            v((2, 16, 128), F32), v((2, NZ, 16, 128), F32),
            v((2, 16, 128), F32), v((2, NY * NX, 16, 128), F32),
            v((2, 16, 128), F32), v((2, 16, 128), F32),
            v((8, M), F32), v((8, M), F32), v((8, M), F32), v((8, M), F32),
            v((2, 16, M), F32), v((2, 16, M), F32), v((32, M), F32), v((32, M), F32),
            v((2, 16, M), F32), v((2, 16, M), F32),
            v((8, 128), F32),
            dma((8,)), regular, regular, dma((7,)), dma((7,)), dma((6,)), dma((6,)), dma((6,)), dma((6,)),
            dma((2,)), dma((2,)), dma((2,)), dma((2,)), dma((2,)), dma((2,)), dma((7,)), dma((7,)),
        ],
        compiler_params=pltpu.CompilerParams(
            collective_id=0, has_side_effects=True, vmem_limit_bytes=60 * 1024 * 1024
        ),
    )(
        right.reshape(CASES, M), schur.reshape(768, 768), modes.reshape(MODES, 1, 768), count,
        order.reshape(1, M), scale.reshape(1, M), loads.reshape(MODES, 1, CASES), coarse,
    )
    return mult.reshape(1, 1, CASES, M), resid.reshape(1, 1, CASES, M)


def solution(mesh):
    field = P("sub", "cluster", None, None)
    return jax.shard_map(
        shards,
        mesh=mesh,
        in_specs=(
            field, field, field, P("sub", "cluster"), P("sub", "cluster", None),
            P("sub", "cluster", None), field, P(("cluster", "sub"), None),
        ),
        out_specs=(field, field),
        check_vma=False,
    )
```

```python
import functools

import jax
import jax.numpy as jnp
from jax import lax
from jax.experimental import pallas as pl
from jax.experimental.pallas import tpu as pltpu
from jax.sharding import PartitionSpec as P

MESH = pl.DeviceIdType.MESH
CHAIN = 32
NZ = 8
NY = 4
NX = 4
NC = 1536
CASES = 16
M = 384
MODES = 6
F32 = jnp.float32
BF16 = jnp.bfloat16
NN = (((1,), (0,)), ((), ()))
NT = (((1,), (1,)), ((), ()))
TN = (((0,), (0,)), ((), ()))


def parts(v):
    high = v.astype(BF16)
    return high, (v - high.astype(F32)).astype(BF16)


def mul(a, b, dims=NN):
    return lax.dot_general(a, b, dims, preferred_element_type=F32)


def mul3(a, b, dims=NN):
    ah, al = parts(a)
    bh, bl = parts(b)
    n = a.shape[0]
    both = mul(jnp.concatenate([ah, al], axis=0), bh, dims)
    return both[:n] + both[n:] + mul(ah, bl, dims)


def mulw(a, wh, wl):
    ah, al = parts(a)
    n = a.shape[0]
    both = mul(jnp.concatenate([ah, al], axis=0), wh)
    return both[:n] + both[n:] + mul(ah, wl)


def iota(shape, dim):
    return lax.broadcasted_iota(jnp.int32, shape, dim)


def fold_lanes(v):
    v = v + pltpu.roll(v, 64, 1)
    v = v + pltpu.roll(v, 32, 1)
    return v + pltpu.roll(v, 16, 1)


def eliminate(matrix, right):
    shape = (CASES, 2 * CASES)
    row = iota(shape, 0)
    tile = jnp.concatenate([matrix, right], axis=1)
    for k in range(0, CASES, 2):
        c1 = jnp.broadcast_to(tile[:, k : k + 1], shape)
        c2 = jnp.broadcast_to(tile[:, k + 1 : k + 2], shape)
        r1 = jnp.broadcast_to(tile[k : k + 1, :], shape)
        r2 = jnp.broadcast_to(tile[k + 1 : k + 2, :], shape)
        p11 = jnp.broadcast_to(c1[k : k + 1, :], shape)
        p21 = jnp.broadcast_to(c1[k + 1 : k + 2, :], shape)
        p12 = jnp.broadcast_to(c2[k : k + 1, :], shape)
        p22 = jnp.broadcast_to(c2[k + 1 : k + 2, :], shape)
        factor = p21 / p11
        s2 = (r2 - factor * r1) / (p22 - factor * p12)
        s1 = (r1 - p12 * s2) / p11
        rest = tile - c1 * s1 - c2 * s2
        tile = jnp.where(row == k, s1, jnp.where(row == k + 1, s2, rest))
    return tile[:, CASES:]


def exact(a, b, dims=NN):
    return lax.dot_general(
        a, b, dims, precision=lax.Precision.HIGHEST, preferred_element_type=F32
    )


def ring(distance, size):
    return min(distance, size - distance)


OFFSETS = sorted(
    (
        (dy, dx, dz)
        for dy in (2, 1, 3, 0)
        for dx in (2, 1, 3, 0)
        for dz in (4, 3, 5, 2, 6, 1, 7, 0)
        if dy or dx or dz
    ),
    key=lambda o: -(ring(o[0], NY) + ring(o[1], NX) + ring(o[2], NZ)),
)


FACES = tuple((dy, dx) for dy, dx, dz in OFFSETS if not dz)


def kernel(
    right_hbm, schur_hbm, modes_hbm, count_hbm, order_hbm, scale_hbm, loads_hbm, coarse_hbm,
    both_ref,
    right_ref, modes_ref, count_ref, order_ref, scale_ref, loads_ref, coarse_ref,
    schur_ref, sh_ref, sl_ref, wh_ref, wl_ref, xa_ref,
    cp_ref, crow_ref, ch_ref, cl_ref,
    out_ref, in_ref, pair_out, pair_in,
    gz_out, gz_in, gy_out, gy_in, gc_out, gc_in,
    left_out, left_in, right_out, right_in,
    fwd, fwd_in, wide_back, wide_back_in, back, back_in,
    tmp_ref, line_ref,
    load_sem, line_sems, coarse_ssem, coarse_rsem, send, recv, pair_ssem, pair_rsem,
    gz_ssem, gz_rsem, gy_ssem, gy_rsem, gc_ssem, gc_rsem, nb_ssem, nb_rsem,
):
    j = lax.axis_index("cluster")
    s = lax.axis_index("sub")
    y = j // NZ
    z = j % NZ
    x = s // 2
    core = s % 2
    other = s + 1 - 2 * core
    face = y * NX + x
    place = face * NZ + z

    def chain(d):
        return ((j + d + CHAIN) % CHAIN, s)

    def beside(d):
        return ((j + d + CHAIN) % CHAIN, other)

    ys = [((y + d) % NY) * NZ for d in range(NY)]
    zs = [(z + d) % NZ for d in range(NZ)]
    xs = [((x + d) % NX) * 2 + core for d in range(NX)]

    def peer(dy, dx, dz):
        return (ys[dy] + zs[dz], xs[dx])

    barrier = pltpu.get_barrier_semaphore()

    def greet(device):
        pl.semaphore_signal(barrier, inc=1, device_id=device, device_id_type=MESH)

    for dz in (4, 3, 5, 2, 6, 1, 7):
        greet(peer(0, 0, dz))
    for d in (-2, 2, -1, 1):
        greet(chain(d))
        greet(beside(d))
    for dy, dx in FACES:
        greet(peer(dy, dx, 0))
    greet(beside(0))

    loads = [
        pltpu.make_async_copy(src, dst, load_sem.at[k])
        for k, (src, dst) in enumerate(
            (
                (loads_hbm, loads_ref), (count_hbm, count_ref), (modes_hbm, modes_ref),
                (order_hbm, order_ref), (coarse_hbm, coarse_ref), (schur_hbm, schur_ref),
                (right_hbm, right_ref), (scale_hbm, scale_ref),
            )
        )
    ]
    for copy in loads:
        copy.start()
    for copy in loads[:4]:
        copy.wait()

    count = count_ref[...]
    active = jnp.where(iota((MODES, 1), 0) < count, 1.0, 0.0)
    basis = modes_ref[:, 0, :] * active
    sub8 = iota((8, 128), 0)
    tmp_ref[...] = jnp.zeros((8, 128), F32)
    tmp_ref[0:MODES, 0:CASES] = loads_ref[:, 0, :] * active
    spread = fold_lanes(tmp_ref[...])
    own_loads = jnp.sum(
        jnp.where(iota((8, 128), 1) // CASES == sub8, spread, 0.0), axis=0, keepdims=True
    )
    out_ref[0] = jnp.concatenate([own_loads, jnp.zeros((1, 128), F32)], axis=0)

    hot = jnp.where(iota((M, M), 0) == order_ref[...], 1.0, 0.0).astype(BF16)
    bh, bl = parts(basis[:, :M])
    permuted = -(mul(bh, hot, NT) + mul(bl, hot, NT))
    left_out[...] = jnp.concatenate([permuted, jnp.zeros((2, M), F32)], axis=0)
    right_out[...] = jnp.concatenate([basis[:, M:], jnp.zeros((2, M), F32)], axis=0)

    loads[4].wait()
    chip = iota((NC, 128), 1)
    wanted = (chip // 32) * 384 + (chip % NZ) * 48 + (chip // NZ % NX) * 12
    pick = jnp.where(iota((NC, 128), 0) == wanted, 1.0, 0.0).astype(BF16)
    rows = jnp.concatenate([coarse_ref[...], jnp.zeros((2, NC), F32)], axis=0)
    for c in range(2):
        shifted = []
        for m in range(MODES):
            d = c * MODES + m
            shifted.append(rows if d == 0 else pltpu.roll(rows, NC - d, 1))
        high, low = parts(jnp.concatenate(shifted, axis=0))
        cp_ref[c] = mul(high, pick) + mul(low, pick)

    pl.semaphore_wait(barrier, 31)

    def remote(src, dst, ssem, rsem, device):
        return pltpu.make_async_remote_copy(
            src_ref=src, dst_ref=dst, send_sem=ssem, recv_sem=rsem,
            device_id=device, device_id_type=MESH,
        )

    def neighbour(k, src, dst, d):
        return remote(src, dst, nb_ssem.at[k], nb_rsem.at[k], chain(d))

    def all_wait(ref, count, sem):
        w = ref.at[pl.ds(0, count)]
        pltpu.make_async_copy(w, w, sem).wait()

    line = pl.ds(pl.multiple_of(2 * z, 2), 2)
    for dz in (4, 3, 5, 2, 6, 1, 7):
        remote(out_ref.at[0], line_ref.at[line], line_sems.at[0], line_sems.at[1], peer(0, 0, dz)).start()
    line_ref[line] = out_ref[0]

    left_copy = neighbour(0, left_out, left_in, -1)
    left_copy.start()
    right_copy = neighbour(1, right_out, right_in, 1)
    right_copy.start()
    colour = j % 4
    coarse_copies = []
    for k, d in enumerate((1, -1, -2)):
        coarse_copies.append(
            remote(cp_ref.at[core], crow_ref.at[0, colour], coarse_ssem.at[k], coarse_rsem.at[k], chain(d))
        )
    for k, d in enumerate((1, 0, -1, -2)):
        coarse_copies.append(
            remote(
                cp_ref.at[1 - core], crow_ref.at[1, colour], coarse_ssem.at[3 + k],
                coarse_rsem.at[3 + k], beside(d),
            )
        )

    for copy in coarse_copies:
        copy.start()
    crow_ref[0, colour] = cp_ref[core]

    for copy in loads[5:]:
        copy.wait()

    def split_rows(i, c):
        rows = pl.ds(pl.multiple_of(i * 128, 128), 128)
        high, low = parts(schur_ref[rows, :])
        sh_ref[rows, :] = high
        sl_ref[rows, :] = low
        for ref, part in ((sh_ref, high), (sl_ref, low)):
            ref[rows, 0:M] = (-mul(part[:, :M], hot, NT)).astype(BF16)
        return c

    def split_columns(i, c):
        cols = pl.ds(pl.multiple_of(i * 128, 128), 128)
        for ref in (sh_ref, sl_ref):
            ref[0:M, cols] = (-mul(hot, ref[0:M, cols])).astype(BF16)
        return c

    lax.fori_loop(0, 6, split_rows, 0)
    all_wait(line_ref, 14, line_sems.at[1])
    block = pl.ds(pl.multiple_of(16 * face, 16), 16)
    for dy, dx in FACES:
        remote(line_ref, in_ref.at[0, block], send.at[0], recv.at[0], peer(dy, dx, 0)).start()
    in_ref[0, block] = line_ref[...]
    lax.fori_loop(0, 6, split_columns, 0)

    landing = pl.ds(pl.multiple_of(2 * place, 2), 2)

    def start_send(r, dy, dx, dz):
        remote(out_ref.at[r], in_ref.at[r, landing], send.at[r], recv.at[r], peer(dy, dx, dz)).start()

    def send_own(r):
        in_ref[r, landing] = out_ref[r]

    def send_some(r, offsets):
        for offset in offsets:
            start_send(r, *offset)

    def send_all(r):
        send_some(r, OFFSETS)
        send_own(r)


    first = j > 0
    last = j < CHAIN - 1

    def apply_product(before, own):
        lifted = jnp.concatenate([jnp.where(first, before, 0.0), own], axis=1)
        return mulw(lifted, sh_ref[...], sl_ref[...])

    def apply_send(i, values):
        fwd[i] = values
        copy = neighbour(3 + 2 * i, fwd.at[i], fwd_in.at[i], 1)
        copy.start()
        return copy

    def apply_middle(i, copy, values):
        copy.wait_recv()
        image = apply_product(fwd_in[i], values)
        back[i] = image[:, :M]
        copy_back = neighbour(4 + 2 * i, back.at[i], back_in.at[i], -1)
        copy_back.start()
        return copy_back, image[:, M:]

    def apply_end(i, copy_back, own):
        copy_back.wait_recv()
        return own + jnp.where(last, back_in[i], 0.0)

    left_copy.wait_recv()
    right_copy.wait_recv()
    following = jnp.where(last, left_in[...], 0.0)
    here = pl.ds(pl.multiple_of(colour * 8, 8), 8)
    after = pl.ds(pl.multiple_of(((j + 1) % 4) * 8, 8), 8)
    ahead = pl.ds(pl.multiple_of(((j + 3) % 4) * 8, 8), 8)
    xa_ref[...] = jnp.zeros((32, 768), F32)
    xa_ref[here, 0:M] = right_out[...]
    xa_ref[after, 0:M] = following
    xa_ref[here, M:] = left_out[...]
    xa_ref[ahead, M:] = right_in[...]
    wide_image = apply_product(xa_ref[:, M:], xa_ref[:, 0:M])
    wide_back[...] = wide_image[:, :M]
    wide_copy = neighbour(2, wide_back, wide_back_in, -1)
    wide_copy.start()
    xa_ref[:, M:] = wide_image[:, M:]

    pieces = []
    for block in (right_out[...], following):
        for m in range(MODES):
            pieces.append(jnp.broadcast_to(block[m : m + 1, :], (CASES, M)))
        pieces.append(jnp.zeros((32, M), F32))
    wh, wl = parts(jnp.transpose(jnp.concatenate(pieces, axis=0)))
    wh_ref[...] = wh
    wl_ref[...] = wl

    for copy in coarse_copies:
        copy.wait_recv()
    ch, cl = parts(crow_ref[...].reshape(384, 128))
    column = iota((128, 256), 1)
    chip = column // 2
    spread = chip + (column % 2) * jnp.where(chip % NZ == NZ - 1, 25, 1)
    both = jnp.where(iota((128, 256), 0) == spread, 1.0, 0.0).astype(BF16)
    ch_ref[...] = mul(ch, both).astype(BF16)
    cl_ref[...] = mul(cl, both).astype(BF16)

    own_case = (iota((CASES, 256), 1) % CASES) == iota((CASES, 256), 0)
    slot = iota((MODES, 8, 128), 2) // CASES == iota((MODES, 8, 128), 0)

    def coefficients(r, field):
        product = mulw(field, wh_ref[...], wl_ref[...])
        flat = jnp.sum(jnp.where(own_case, product, 0.0), axis=0, keepdims=True)
        out_ref[r] = jnp.concatenate([flat[:, :128], flat[:, 128:]], axis=0)

    def picked(full, at):
        blocks = [
            jnp.sum(
                jnp.where(slot, full[at + c * 48 : at + (c + 1) * 48].reshape(MODES, 8, 128), 0.0),
                axis=0,
            )
            for c in range(4)
        ]
        return jnp.concatenate(blocks, axis=0)

    def coarse(r):
        all_wait(in_ref.at[r], 254 if r else 240, recv.at[r])
        gh, gl = parts(in_ref[r])
        both = mul(ch_ref[...], jnp.concatenate([gh, gl], axis=1))
        full = both[:, :128] + both[:, 128:] + mul(cl_ref[...], gh)
        pair_out[r] = picked(full, 192)
        copy = remote(pair_out.at[r], pair_in.at[r], pair_ssem.at[r], pair_rsem.at[r], beside(0))
        copy.start()
        mine = picked(full, 0)
        copy.wait_recv()
        turned = jnp.transpose(mine + pair_in[r])
        return jnp.sum(turned.reshape(8, CASES, 32), axis=0)

    def grams(a, blocks):
        spare = jnp.zeros((128 - CASES * len(blocks), M), F32)
        return mul3(a, jnp.concatenate([*blocks, spare], axis=0), NT)

    def gram_z(i, values):
        gz_out[i] = values
        for dz in (4, 3, 5, 2, 6, 1, 7):
            remote(gz_out.at[i], gz_in.at[i, z], gz_ssem.at[i], gz_rsem.at[i], peer(0, 0, dz)).start()
        gz_in[i, z] = values

    def gram_y(i):
        all_wait(gz_in.at[i], NZ - 1, gz_rsem.at[i])
        values = jnp.sum(gz_in[i], axis=0)
        gy_out[i] = values
        for dy, dx in FACES:
            remote(
                gy_out.at[i], gy_in.at[i, face], gy_ssem.at[i], gy_rsem.at[i], peer(dy, dx, 0)
            ).start()
        gy_in[i, face] = values

    def gram_pair(i):
        all_wait(gy_in.at[i], NY * NX - 1, gy_rsem.at[i])
        values = jnp.sum(gy_in[i], axis=0)
        gc_out[i] = values
        copy = remote(gc_out.at[i], gc_in.at[i], gc_ssem.at[i], gc_rsem.at[i], beside(0))
        copy.start()
        return copy, values

    def gram_end(i, copy, values):
        copy.wait_recv()
        return values + gc_in[i]

    right = right_ref[...]
    scale = scale_ref[...]
    y0 = coarse(0)
    wide_copy.wait_recv()
    xa_ref[:, M:] = xa_ref[:, M:] + jnp.where(last, wide_back_in[...], 0.0)
    moved = mul3(y0, xa_ref[...])
    mult = moved[:, :M]
    tt = right - moved[:, M:]

    coefficients(1, tt)
    send_all(1)
    resid = tt - mul3(coarse(1), xa_ref[:, 0:M])
    scaled = scale * resid

    coefficients(2, scaled)
    copy = apply_send(0, scaled)
    send_all(2)
    copy_back, own = apply_middle(0, copy, scaled)
    y2 = coarse(2)
    p = apply_end(0, copy_back, own)
    moved = mul3(y2, xa_ref[...])
    a = scaled - moved[:, :M]
    p = p - moved[:, M:]

    coefficients(3, p)
    send_all(3)
    q = p - mul3(coarse(3), xa_ref[:, 0:M])
    scaled = scale * q

    coefficients(4, scaled)
    copy = apply_send(1, scaled)
    send_all(4)
    gram_z(0, grams(a, (p, resid, q)))
    copy_back, own = apply_middle(1, copy, scaled)
    y4 = coarse(4)
    u = apply_end(1, copy_back, own)
    moved = mul3(y4, xa_ref[...])
    w = scaled - moved[:, :M]
    u = u - moved[:, M:]

    gram_z(1, grams(w, (p, u, resid, q)))
    coefficients(5, u)
    send_some(5, OFFSETS[:48])
    gram_y(0)
    send_some(5, OFFSETS[48:100])
    gram_y(1)
    send_some(5, OFFSETS[100:])
    send_own(5)
    copy, values = gram_pair(0)
    sums = gram_end(0, copy, values)
    ap, ar, aq = (sums[:, k * CASES : (k + 1) * CASES] for k in range(3))
    eye = jnp.where(iota((CASES, CASES), 0) == iota((CASES, CASES), 1), 1.0, 0.0)
    inverse = eliminate(ap, eye)
    alpha = exact(inverse, ar)
    rest = ar - exact(aq, alpha)
    v = u - mul3(coarse(5), xa_ref[:, 0:M])
    aq_fields = jnp.concatenate([a, q], axis=1)
    first_step = exact(alpha, aq_fields, TN)
    copy, values = gram_pair(1)
    sums = gram_end(1, copy, values)
    wp, wu, wr, wq = (sums[:, k * CASES : (k + 1) * CASES] for k in range(4))
    across = exact(inverse, wp, NT)
    right_side = wr - exact(wq, alpha) - exact(across, rest, TN)
    gamma = eliminate(wu - exact(wp, across), right_side)
    turned = jnp.concatenate([w, v], axis=1) - exact(across, aq_fields, TN)
    mixed = first_step + exact(gamma, turned, TN)
    both_ref[0:CASES] = mult + mixed[:, :M]
    both_ref[CASES:] = resid - mixed[:, M:]

    left_copy.wait_send()
    right_copy.wait_send()
    all_wait(line_ref, 14, line_sems.at[0])
    for copy in coarse_copies:
        copy.wait_send()
    pltpu.make_async_copy(wide_back, wide_back, nb_ssem.at[2]).wait()
    for i in range(2):
        pltpu.make_async_copy(fwd.at[i], fwd.at[i], nb_ssem.at[3 + 2 * i]).wait()
        pltpu.make_async_copy(back.at[i], back.at[i], nb_ssem.at[4 + 2 * i]).wait()
        all_wait(gz_in.at[i], NZ - 1, gz_ssem.at[i])
        all_wait(gy_in.at[i], NY * NX - 1, gy_ssem.at[i])
        pltpu.make_async_copy(gc_out.at[i], gc_out.at[i], gc_ssem.at[i]).wait()
    for r in range(6):
        all_wait(in_ref.at[r], 254 if r else 240, send.at[r])
        pltpu.make_async_copy(pair_out.at[r], pair_out.at[r], pair_ssem.at[r]).wait()


def shards(right, schur, modes, count, order, scale, loads, coarse):
    vmem = pl.BlockSpec(memory_space=pltpu.VMEM)
    dma = pltpu.SemaphoreType.DMA
    v = pltpu.VMEM
    both = pl.pallas_call(
        kernel,
        name="feti",
        out_shape=jax.ShapeDtypeStruct((2 * CASES, M), F32),
        in_specs=[pl.BlockSpec(memory_space=pltpu.HBM)] * 8,
        out_specs=vmem,
        scratch_shapes=[
            v((CASES, M), F32), v((MODES, 1, 768), F32), v((1, 1), jnp.int32), v((1, M), jnp.int32),
            v((1, M), F32), v((MODES, 1, CASES), F32), v((MODES, NC), F32),
            v((768, 768), F32), v((768, 768), BF16), v((768, 768), BF16),
            v((M, 256), BF16), v((M, 256), BF16), v((32, 768), F32),
            v((2, 48, 128), F32), v((2, 4, 48, 128), F32), v((384, 256), BF16), v((384, 256), BF16),
            v((6, 2, 128), F32), v((6, 256, 128), F32), v((6, 32, 128), F32), v((6, 32, 128), F32),
            v((2, 16, 128), F32), v((2, NZ, 16, 128), F32),
            v((2, 16, 128), F32), v((2, NY * NX, 16, 128), F32),
            v((2, 16, 128), F32), v((2, 16, 128), F32),
            v((8, M), F32), v((8, M), F32), v((8, M), F32), v((8, M), F32),
            v((2, 16, M), F32), v((2, 16, M), F32), v((32, M), F32), v((32, M), F32),
            v((2, 16, M), F32), v((2, 16, M), F32),
            v((8, 128), F32), v((16, 128), F32),
            dma((8,)), dma((2,)), dma((7,)), dma((7,)), dma((6,)), dma((6,)), dma((6,)), dma((6,)),
            dma((2,)), dma((2,)), dma((2,)), dma((2,)), dma((2,)), dma((2,)), dma((7,)), dma((7,)),
        ],
        compiler_params=pltpu.CompilerParams(
            collective_id=0, has_side_effects=True, vmem_limit_bytes=60 * 1024 * 1024
        ),
    )(
        right.reshape(CASES, M), schur.reshape(768, 768), modes.reshape(MODES, 1, 768), count,
        order.reshape(1, M), scale.reshape(1, M), loads.reshape(MODES, 1, CASES), coarse,
    )
    return both[:CASES].reshape(1, 1, CASES, M), both[CASES:].reshape(1, 1, CASES, M)


def solution(mesh):
    field = P("sub", "cluster", None, None)
    return jax.shard_map(
        shards,
        mesh=mesh,
        in_specs=(
            field, field, field, P("sub", "cluster"), P("sub", "cluster", None),
            P("sub", "cluster", None), field, P(("cluster", "sub"), None),
        ),
        out_specs=(field, field),
        check_vma=False,
    )
```

```python
import functools

import jax
import jax.numpy as jnp
from jax import lax
from jax.experimental import pallas as pl
from jax.experimental.pallas import tpu as pltpu
from jax.sharding import PartitionSpec as P

MESH = pl.DeviceIdType.MESH
CHAIN = 32
NZ = 8
NY = 4
NX = 4
NC = 1536
CASES = 16
M = 384
MODES = 6
F32 = jnp.float32
BF16 = jnp.bfloat16
NN = (((1,), (0,)), ((), ()))
NT = (((1,), (1,)), ((), ()))
TN = (((0,), (0,)), ((), ()))


def parts(v):
    high = v.astype(BF16)
    return high, (v - high.astype(F32)).astype(BF16)


def mul(a, b, dims=NN):
    return lax.dot_general(a, b, dims, preferred_element_type=F32)


def mul3(a, b, dims=NN):
    ah, al = parts(a)
    bh, bl = parts(b)
    n = a.shape[0]
    both = mul(jnp.concatenate([ah, al], axis=0), bh, dims)
    return both[:n] + both[n:] + mul(ah, bl, dims)


def mulw(a, wh, wl):
    ah, al = parts(a)
    n = a.shape[0]
    both = mul(jnp.concatenate([ah, al], axis=0), wh)
    return both[:n] + both[n:] + mul(ah, wl)


def iota(shape, dim):
    return lax.broadcasted_iota(jnp.int32, shape, dim)


def fold_lanes(v):
    v = v + pltpu.roll(v, 64, 1)
    v = v + pltpu.roll(v, 32, 1)
    return v + pltpu.roll(v, 16, 1)


def eliminate(matrix, right):
    shape = (CASES, 2 * CASES)
    row = iota(shape, 0)
    tile = jnp.concatenate([matrix, right], axis=1)
    for k in range(0, CASES, 2):
        c1 = jnp.broadcast_to(tile[:, k : k + 1], shape)
        c2 = jnp.broadcast_to(tile[:, k + 1 : k + 2], shape)
        r1 = jnp.broadcast_to(tile[k : k + 1, :], shape)
        r2 = jnp.broadcast_to(tile[k + 1 : k + 2, :], shape)
        p11 = jnp.broadcast_to(c1[k : k + 1, :], shape)
        p21 = jnp.broadcast_to(c1[k + 1 : k + 2, :], shape)
        p12 = jnp.broadcast_to(c2[k : k + 1, :], shape)
        p22 = jnp.broadcast_to(c2[k + 1 : k + 2, :], shape)
        factor = p21 / p11
        s2 = (r2 - factor * r1) / (p22 - factor * p12)
        s1 = (r1 - p12 * s2) / p11
        rest = tile - c1 * s1 - c2 * s2
        tile = jnp.where(row == k, s1, jnp.where(row == k + 1, s2, rest))
    return tile[:, CASES:]


def exact(a, b, dims=NN):
    return lax.dot_general(
        a, b, dims, precision=lax.Precision.HIGHEST, preferred_element_type=F32
    )


def ring(distance, size):
    return min(distance, size - distance)


OFFSETS = sorted(
    (
        (dy, dx, dz)
        for dy in (2, 1, 3, 0)
        for dx in (2, 1, 3, 0)
        for dz in (4, 3, 5, 2, 6, 1, 7, 0)
        if dy or dx or dz
    ),
    key=lambda o: -(ring(o[0], NY) + ring(o[1], NX) + ring(o[2], NZ)),
)


FACES = tuple((dy, dx) for dy, dx, dz in OFFSETS if not dz)


def kernel(
    right_hbm, schur_hbm, modes_hbm, count_hbm, order_hbm, scale_hbm, loads_hbm, coarse_hbm,
    both_ref,
    right_ref, modes_ref, count_ref, order_ref, scale_ref, loads_ref, coarse_ref,
    schur_ref, sh_ref, sl_ref, wh_ref, wl_ref, xa_ref,
    cp_ref, crow_ref, ch_ref, cl_ref,
    out_ref, in_ref, pair_out, pair_in,
    gz_out, gz_in, gy_out, gy_in, gc_out, gc_in,
    left_out, left_in, right_out, right_in,
    fwd, fwd_in, wide_back, wide_back_in, back, back_in,
    tmp_ref, line_ref,
    load_sem, line_sems, coarse_ssem, coarse_rsem, send, recv, pair_ssem, pair_rsem,
    gz_ssem, gz_rsem, gy_ssem, gy_rsem, gc_ssem, gc_rsem, nb_ssem, nb_rsem,
):
    j = lax.axis_index("cluster")
    s = lax.axis_index("sub")
    y = j // NZ
    z = j % NZ
    x = s // 2
    core = s % 2
    other = s + 1 - 2 * core
    face = y * NX + x
    place = face * NZ + z

    def chain(d):
        return ((j + d + CHAIN) % CHAIN, s)

    def beside(d):
        return ((j + d + CHAIN) % CHAIN, other)

    ys = [((y + d) % NY) * NZ for d in range(NY)]
    zs = [(z + d) % NZ for d in range(NZ)]
    xs = [((x + d) % NX) * 2 + core for d in range(NX)]

    def peer(dy, dx, dz):
        return (ys[dy] + zs[dz], xs[dx])

    barrier = pltpu.get_barrier_semaphore()

    def greet(device):
        pl.semaphore_signal(barrier, inc=1, device_id=device, device_id_type=MESH)

    for dz in (4, 3, 5, 2, 6, 1, 7):
        greet(peer(0, 0, dz))
    for d in (-2, 2, -1, 1):
        greet(chain(d))
        greet(beside(d))
    for dy, dx in FACES:
        greet(peer(dy, dx, 0))
    greet(beside(0))

    loads = [
        pltpu.make_async_copy(src, dst, load_sem.at[k])
        for k, (src, dst) in enumerate(
            (
                (loads_hbm, loads_ref), (count_hbm, count_ref), (modes_hbm, modes_ref),
                (order_hbm, order_ref), (coarse_hbm, coarse_ref), (schur_hbm, schur_ref),
                (right_hbm, right_ref), (scale_hbm, scale_ref),
            )
        )
    ]
    for copy in loads:
        copy.start()
    for copy in loads[:4]:
        copy.wait()

    count = count_ref[...]
    active = jnp.where(iota((MODES, 1), 0) < count, 1.0, 0.0)
    basis = modes_ref[:, 0, :] * active
    sub8 = iota((8, 128), 0)
    tmp_ref[...] = jnp.zeros((8, 128), F32)
    tmp_ref[0:MODES, 0:CASES] = loads_ref[:, 0, :] * active
    spread = fold_lanes(tmp_ref[...])
    own_loads = jnp.sum(
        jnp.where(iota((8, 128), 1) // CASES == sub8, spread, 0.0), axis=0, keepdims=True
    )
    out_ref[0] = jnp.concatenate([own_loads, jnp.zeros((1, 128), F32)], axis=0)

    hot = jnp.where(iota((M, M), 0) == order_ref[...], 1.0, 0.0).astype(BF16)
    bh, bl = parts(basis[:, :M])
    permuted = -(mul(bh, hot, NT) + mul(bl, hot, NT))
    left_out[...] = jnp.concatenate([permuted, jnp.zeros((2, M), F32)], axis=0)
    right_out[...] = jnp.concatenate([basis[:, M:], jnp.zeros((2, M), F32)], axis=0)

    loads[4].wait()
    chip = iota((NC, 128), 1)
    wanted = (chip // 32) * 384 + (chip % NZ) * 48 + (chip // NZ % NX) * 12
    pick = jnp.where(iota((NC, 128), 0) == wanted, 1.0, 0.0).astype(BF16)
    rows = jnp.concatenate([coarse_ref[...], jnp.zeros((2, NC), F32)], axis=0)
    for c in range(2):
        shifted = []
        for m in range(MODES):
            d = c * MODES + m
            shifted.append(rows if d == 0 else pltpu.roll(rows, NC - d, 1))
        high, low = parts(jnp.concatenate(shifted, axis=0))
        cp_ref[c] = mul(high, pick) + mul(low, pick)

    pl.semaphore_wait(barrier, 31)

    def remote(src, dst, ssem, rsem, device):
        return pltpu.make_async_remote_copy(
            src_ref=src, dst_ref=dst, send_sem=ssem, recv_sem=rsem,
            device_id=device, device_id_type=MESH,
        )

    def neighbour(k, src, dst, d):
        return remote(src, dst, nb_ssem.at[k], nb_rsem.at[k], chain(d))

    def all_wait(ref, count, sem):
        w = ref.at[pl.ds(0, count)]
        pltpu.make_async_copy(w, w, sem).wait()

    line = pl.ds(pl.multiple_of(2 * z, 2), 2)
    for dz in (4, 3, 5, 2, 6, 1, 7):
        remote(out_ref.at[0], line_ref.at[line], line_sems.at[0], line_sems.at[1], peer(0, 0, dz)).start()
    line_ref[line] = out_ref[0]

    left_copy = neighbour(0, left_out, left_in, -1)
    left_copy.start()
    right_copy = neighbour(1, right_out, right_in, 1)
    right_copy.start()
    colour = j % 4
    coarse_copies = []
    for k, d in enumerate((1, -1, -2)):
        coarse_copies.append(
            remote(cp_ref.at[core], crow_ref.at[0, colour], coarse_ssem.at[k], coarse_rsem.at[k], chain(d))
        )
    for k, d in enumerate((1, 0, -1, -2)):
        coarse_copies.append(
            remote(
                cp_ref.at[1 - core], crow_ref.at[1, colour], coarse_ssem.at[3 + k],
                coarse_rsem.at[3 + k], beside(d),
            )
        )

    for copy in coarse_copies:
        copy.start()
    crow_ref[0, colour] = cp_ref[core]

    for copy in loads[5:]:
        copy.wait()

    def split_rows(i, c):
        rows = pl.ds(pl.multiple_of(i * 128, 128), 128)
        high, low = parts(schur_ref[rows, :])
        sh_ref[rows, :] = high
        sl_ref[rows, :] = low
        for ref, part in ((sh_ref, high), (sl_ref, low)):
            ref[rows, 0:M] = (-mul(part[:, :M], hot, NT)).astype(BF16)
        return c

    def split_columns(i, c):
        cols = pl.ds(pl.multiple_of(i * 128, 128), 128)
        for ref in (sh_ref, sl_ref):
            ref[0:M, cols] = (-mul(hot, ref[0:M, cols])).astype(BF16)
        return c

    lax.fori_loop(0, 6, split_rows, 0)
    all_wait(line_ref, 14, line_sems.at[1])
    block = pl.ds(pl.multiple_of(16 * face, 16), 16)
    for dy, dx in FACES:
        remote(line_ref, in_ref.at[0, block], send.at[0], recv.at[0], peer(dy, dx, 0)).start()
    in_ref[0, block] = line_ref[...]
    lax.fori_loop(0, 6, split_columns, 0)

    landing = pl.ds(pl.multiple_of(2 * place, 2), 2)

    def start_send(r, dy, dx, dz):
        remote(out_ref.at[r], in_ref.at[r, landing], send.at[r], recv.at[r], peer(dy, dx, dz)).start()

    def send_own(r):
        in_ref[r, landing] = out_ref[r]

    def send_some(r, offsets):
        for offset in offsets:
            start_send(r, *offset)

    def send_all(r):
        send_some(r, OFFSETS)
        send_own(r)


    first = j > 0
    last = j < CHAIN - 1

    def apply_product(before, own):
        lifted = jnp.concatenate([jnp.where(first, before, 0.0), own], axis=1)
        return mulw(lifted, sh_ref[...], sl_ref[...])

    def apply_send(i, values):
        fwd[i] = values
        copy = neighbour(3 + 2 * i, fwd.at[i], fwd_in.at[i], 1)
        copy.start()
        return copy

    def apply_middle(i, copy, values):
        copy.wait_recv()
        image = apply_product(fwd_in[i], values)
        back[i] = image[:, :M]
        copy_back = neighbour(4 + 2 * i, back.at[i], back_in.at[i], -1)
        copy_back.start()
        return copy_back, image[:, M:]

    def apply_end(i, copy_back, own):
        copy_back.wait_recv()
        return own + jnp.where(last, back_in[i], 0.0)

    left_copy.wait_recv()
    right_copy.wait_recv()
    following = jnp.where(last, left_in[...], 0.0)
    here = pl.ds(pl.multiple_of(colour * 8, 8), 8)
    after = pl.ds(pl.multiple_of(((j + 1) % 4) * 8, 8), 8)
    ahead = pl.ds(pl.multiple_of(((j + 3) % 4) * 8, 8), 8)
    xa_ref[...] = jnp.zeros((32, 768), F32)
    xa_ref[here, 0:M] = right_out[...]
    xa_ref[after, 0:M] = following
    xa_ref[here, M:] = left_out[...]
    xa_ref[ahead, M:] = right_in[...]
    wide_image = apply_product(xa_ref[:, M:], xa_ref[:, 0:M])
    wide_back[...] = wide_image[:, :M]
    wide_copy = neighbour(2, wide_back, wide_back_in, -1)
    wide_copy.start()
    xa_ref[:, M:] = wide_image[:, M:]

    pieces = []
    for block in (right_out[...], following):
        for m in range(MODES):
            pieces.append(jnp.broadcast_to(block[m : m + 1, :], (CASES, M)))
        pieces.append(jnp.zeros((32, M), F32))
    wh, wl = parts(jnp.transpose(jnp.concatenate(pieces, axis=0)))
    wh_ref[...] = wh
    wl_ref[...] = wl

    for copy in coarse_copies:
        copy.wait_recv()
    ch, cl = parts(crow_ref[...].reshape(384, 128))
    column = iota((128, 256), 1)
    chip = column // 2
    spread = chip + (column % 2) * jnp.where(chip % NZ == NZ - 1, 25, 1)
    both = jnp.where(iota((128, 256), 0) == spread, 1.0, 0.0).astype(BF16)
    ch_ref[...] = mul(ch, both).astype(BF16)
    cl_ref[...] = mul(cl, both).astype(BF16)

    own_case = (iota((CASES, 256), 1) % CASES) == iota((CASES, 256), 0)
    slot = iota((MODES, 8, 128), 2) // CASES == iota((MODES, 8, 128), 0)

    def coefficients(r, field):
        product = mulw(field, wh_ref[...], wl_ref[...])
        flat = jnp.sum(jnp.where(own_case, product, 0.0), axis=0, keepdims=True)
        out_ref[r] = jnp.concatenate([flat[:, :128], flat[:, 128:]], axis=0)

    def picked(full, at):
        blocks = [
            jnp.sum(
                jnp.where(slot, full[at + c * 48 : at + (c + 1) * 48].reshape(MODES, 8, 128), 0.0),
                axis=0,
            )
            for c in range(4)
        ]
        return jnp.concatenate(blocks, axis=0)

    def coarse(r):
        all_wait(in_ref.at[r], 254 if r else 240, recv.at[r])
        gh, gl = parts(in_ref[r])
        both = mul(ch_ref[...], jnp.concatenate([gh, gl], axis=1))
        full = both[:, :128] + both[:, 128:] + mul(cl_ref[...], gh)
        pair_out[r] = picked(full, 192)
        copy = remote(pair_out.at[r], pair_in.at[r], pair_ssem.at[r], pair_rsem.at[r], beside(0))
        copy.start()
        mine = picked(full, 0)
        copy.wait_recv()
        turned = jnp.transpose(mine + pair_in[r])
        return jnp.sum(turned.reshape(8, CASES, 32), axis=0)

    def grams(a, blocks):
        spare = jnp.zeros((128 - CASES * len(blocks), M), F32)
        return mul3(a, jnp.concatenate([*blocks, spare], axis=0), NT)

    def gram_z(i, values):
        gz_out[i] = values
        for dz in (4, 3, 5, 2, 6, 1, 7):
            remote(gz_out.at[i], gz_in.at[i, z], gz_ssem.at[i], gz_rsem.at[i], peer(0, 0, dz)).start()
        gz_in[i, z] = values

    def gram_y(i):
        all_wait(gz_in.at[i], NZ - 1, gz_rsem.at[i])
        values = jnp.sum(gz_in[i], axis=0)
        gy_out[i] = values
        for dy, dx in FACES:
            remote(
                gy_out.at[i], gy_in.at[i, face], gy_ssem.at[i], gy_rsem.at[i], peer(dy, dx, 0)
            ).start()
        gy_in[i, face] = values

    def gram_pair(i):
        all_wait(gy_in.at[i], NY * NX - 1, gy_rsem.at[i])
        values = jnp.sum(gy_in[i], axis=0)
        gc_out[i] = values
        copy = remote(gc_out.at[i], gc_in.at[i], gc_ssem.at[i], gc_rsem.at[i], beside(0))
        copy.start()
        return copy, values

    def gram_end(i, copy, values):
        copy.wait_recv()
        return values + gc_in[i]

    right = right_ref[...]
    scale = scale_ref[...]
    y0 = coarse(0)
    wide_copy.wait_recv()
    xa_ref[:, M:] = xa_ref[:, M:] + jnp.where(last, wide_back_in[...], 0.0)
    xh, xl = parts(xa_ref[...])
    moved = mulw(y0, xh, xl)
    mult = moved[:, :M]
    tt = right - moved[:, M:]

    coefficients(1, tt)
    send_all(1)
    resid = tt - mulw(coarse(1), xh[:, :M], xl[:, :M])
    scaled = scale * resid

    coefficients(2, scaled)
    copy = apply_send(0, scaled)
    send_all(2)
    copy_back, own = apply_middle(0, copy, scaled)
    y2 = coarse(2)
    p = apply_end(0, copy_back, own)
    moved = mulw(y2, xh, xl)
    a = scaled - moved[:, :M]
    p = p - moved[:, M:]

    coefficients(3, p)
    send_all(3)
    q = p - mulw(coarse(3), xh[:, :M], xl[:, :M])
    scaled = scale * q

    coefficients(4, scaled)
    copy = apply_send(1, scaled)
    send_all(4)
    copy_back, own = apply_middle(1, copy, scaled)
    gram_z(0, grams(a, (p, resid, q)))
    y4 = coarse(4)
    u = apply_end(1, copy_back, own)
    moved = mulw(y4, xh, xl)
    w = scaled - moved[:, :M]
    u = u - moved[:, M:]

    gram_z(1, grams(w, (p, u, resid, q)))
    coefficients(5, u)
    send_some(5, OFFSETS[:48])
    gram_y(0)
    send_some(5, OFFSETS[48:100])
    gram_y(1)
    send_some(5, OFFSETS[100:])
    send_own(5)
    copy, values = gram_pair(0)
    sums = gram_end(0, copy, values)
    ap, ar, aq = (sums[:, k * CASES : (k + 1) * CASES] for k in range(3))
    eye = jnp.where(iota((CASES, CASES), 0) == iota((CASES, CASES), 1), 1.0, 0.0)
    inverse = eliminate(ap, eye)
    alpha = exact(inverse, ar)
    rest = ar - exact(aq, alpha)
    v = u - mulw(coarse(5), xh[:, :M], xl[:, :M])
    aq_fields = jnp.concatenate([a, q], axis=1)
    first_step = exact(alpha, aq_fields, TN)
    copy, values = gram_pair(1)
    sums = gram_end(1, copy, values)
    wp, wu, wr, wq = (sums[:, k * CASES : (k + 1) * CASES] for k in range(4))
    across = exact(inverse, wp, NT)
    right_side = wr - exact(wq, alpha) - exact(across, rest, TN)
    gamma = eliminate(wu - exact(wp, across), right_side)
    turned = jnp.concatenate([w, v], axis=1) - exact(across, aq_fields, TN)
    mixed = first_step + exact(gamma, turned, TN)
    both_ref[0:CASES] = mult + mixed[:, :M]
    both_ref[CASES:] = resid - mixed[:, M:]

    left_copy.wait_send()
    right_copy.wait_send()
    all_wait(line_ref, 14, line_sems.at[0])
    for copy in coarse_copies:
        copy.wait_send()
    pltpu.make_async_copy(wide_back, wide_back, nb_ssem.at[2]).wait()
    for i in range(2):
        pltpu.make_async_copy(fwd.at[i], fwd.at[i], nb_ssem.at[3 + 2 * i]).wait()
        pltpu.make_async_copy(back.at[i], back.at[i], nb_ssem.at[4 + 2 * i]).wait()
        all_wait(gz_in.at[i], NZ - 1, gz_ssem.at[i])
        all_wait(gy_in.at[i], NY * NX - 1, gy_ssem.at[i])
        pltpu.make_async_copy(gc_out.at[i], gc_out.at[i], gc_ssem.at[i]).wait()
    for r in range(6):
        all_wait(in_ref.at[r], 254 if r else 240, send.at[r])
        pltpu.make_async_copy(pair_out.at[r], pair_out.at[r], pair_ssem.at[r]).wait()


def shards(right, schur, modes, count, order, scale, loads, coarse):
    vmem = pl.BlockSpec(memory_space=pltpu.VMEM)
    dma = pltpu.SemaphoreType.DMA
    v = pltpu.VMEM
    both = pl.pallas_call(
        kernel,
        name="feti",
        out_shape=jax.ShapeDtypeStruct((2 * CASES, M), F32),
        in_specs=[pl.BlockSpec(memory_space=pltpu.HBM)] * 8,
        out_specs=vmem,
        scratch_shapes=[
            v((CASES, M), F32), v((MODES, 1, 768), F32), v((1, 1), jnp.int32), v((1, M), jnp.int32),
            v((1, M), F32), v((MODES, 1, CASES), F32), v((MODES, NC), F32),
            v((768, 768), F32), v((768, 768), BF16), v((768, 768), BF16),
            v((M, 256), BF16), v((M, 256), BF16), v((32, 768), F32),
            v((2, 48, 128), F32), v((2, 4, 48, 128), F32), v((384, 256), BF16), v((384, 256), BF16),
            v((6, 2, 128), F32), v((6, 256, 128), F32), v((6, 32, 128), F32), v((6, 32, 128), F32),
            v((2, 16, 128), F32), v((2, NZ, 16, 128), F32),
            v((2, 16, 128), F32), v((2, NY * NX, 16, 128), F32),
            v((2, 16, 128), F32), v((2, 16, 128), F32),
            v((8, M), F32), v((8, M), F32), v((8, M), F32), v((8, M), F32),
            v((2, 16, M), F32), v((2, 16, M), F32), v((32, M), F32), v((32, M), F32),
            v((2, 16, M), F32), v((2, 16, M), F32),
            v((8, 128), F32), v((16, 128), F32),
            dma((8,)), dma((2,)), dma((7,)), dma((7,)), dma((6,)), dma((6,)), dma((6,)), dma((6,)),
            dma((2,)), dma((2,)), dma((2,)), dma((2,)), dma((2,)), dma((2,)), dma((7,)), dma((7,)),
        ],
        compiler_params=pltpu.CompilerParams(
            collective_id=0, has_side_effects=True, vmem_limit_bytes=60 * 1024 * 1024
        ),
    )(
        right.reshape(CASES, M), schur.reshape(768, 768), modes.reshape(MODES, 1, 768), count,
        order.reshape(1, M), scale.reshape(1, M), loads.reshape(MODES, 1, CASES), coarse,
    )
    return both[:CASES].reshape(1, 1, CASES, M), both[CASES:].reshape(1, 1, CASES, M)


def solution(mesh):
    field = P("sub", "cluster", None, None)
    return jax.shard_map(
        shards,
        mesh=mesh,
        in_specs=(
            field, field, field, P("sub", "cluster"), P("sub", "cluster", None),
            P("sub", "cluster", None), field, P(("cluster", "sub"), None),
        ),
        out_specs=(field, field),
        check_vma=False,
    )
```

```python
import functools

import jax
import jax.numpy as jnp
from jax import lax
from jax.experimental import pallas as pl
from jax.experimental.pallas import tpu as pltpu
from jax.sharding import PartitionSpec as P

MESH = pl.DeviceIdType.MESH
CHAIN = 32
NZ = 8
NY = 4
NX = 4
NC = 1536
CASES = 16
M = 384
MODES = 6
F32 = jnp.float32
BF16 = jnp.bfloat16
NN = (((1,), (0,)), ((), ()))
NT = (((1,), (1,)), ((), ()))
TN = (((0,), (0,)), ((), ()))


def parts(v):
    high = v.astype(BF16)
    return high, (v - high.astype(F32)).astype(BF16)


def mul(a, b, dims=NN):
    return lax.dot_general(a, b, dims, preferred_element_type=F32)


def mul3(a, b, dims=NN):
    ah, al = parts(a)
    bh, bl = parts(b)
    n = a.shape[0]
    both = mul(jnp.concatenate([ah, al], axis=0), bh, dims)
    return both[:n] + both[n:] + mul(ah, bl, dims)


def mulw(a, wh, wl):
    ah, al = parts(a)
    n = a.shape[0]
    both = mul(jnp.concatenate([ah, al], axis=0), wh)
    return both[:n] + both[n:] + mul(ah, wl)


def iota(shape, dim):
    return lax.broadcasted_iota(jnp.int32, shape, dim)


def fold_lanes(v):
    v = v + pltpu.roll(v, 64, 1)
    v = v + pltpu.roll(v, 32, 1)
    return v + pltpu.roll(v, 16, 1)


def eliminate(matrix, right):
    shape = (CASES, 2 * CASES)
    row = iota(shape, 0)
    tile = jnp.concatenate([matrix, right], axis=1)
    for k in range(0, CASES, 4):
        c = [jnp.broadcast_to(tile[:, k + i : k + i + 1], shape) for i in range(4)]
        r = [jnp.broadcast_to(tile[k + i : k + i + 1, :], shape) for i in range(4)]
        p = [[jnp.broadcast_to(c[n][k + i : k + i + 1, :], shape) for n in range(4)] for i in range(4)]
        for i in range(4):
            factor = 1.0 / p[i][i]
            r[i] = r[i] * factor
            for n in range(i + 1, 4):
                p[i][n] = p[i][n] * factor
            for o in range(4):
                if o != i:
                    r[o] = r[o] - p[o][i] * r[i]
                    for n in range(i + 1, 4):
                        p[o][n] = p[o][n] - p[o][i] * p[i][n]
        rest = tile - (c[0] * r[0] + c[1] * r[1]) - (c[2] * r[2] + c[3] * r[3])
        for i in range(4):
            rest = jnp.where(row == k + i, r[i], rest)
        tile = rest
    return tile[:, CASES:]


def exact(a, b, dims=NN):
    return lax.dot_general(
        a, b, dims, precision=lax.Precision.HIGHEST, preferred_element_type=F32
    )


def ring(distance, size):
    return min(distance, size - distance)


OFFSETS = sorted(
    (
        (dy, dx, dz)
        for dy in (2, 1, 3, 0)
        for dx in (2, 1, 3, 0)
        for dz in (4, 3, 5, 2, 6, 1, 7, 0)
        if dy or dx or dz
    ),
    key=lambda o: -(ring(o[0], NY) + ring(o[1], NX) + ring(o[2], NZ)),
)


FACES = tuple((dy, dx) for dy, dx, dz in OFFSETS if not dz)


def kernel(
    right_hbm, schur_hbm, modes_hbm, count_hbm, order_hbm, scale_hbm, loads_hbm, coarse_hbm,
    both_ref,
    right_ref, modes_ref, count_ref, order_ref, scale_ref, loads_ref, coarse_ref,
    schur_ref, sh_ref, sl_ref, wh_ref, wl_ref, xa_ref,
    cp_ref, crow_ref, ch_ref, cl_ref,
    out_ref, in_ref, pair_out, pair_in,
    gz_out, gz_in, gy_out, gy_in, gc_out, gc_in,
    left_out, left_in, right_out, right_in,
    fwd, fwd_in, wide_back, wide_back_in, back, back_in,
    tmp_ref, line_ref,
    load_sem, line_sems, coarse_ssem, coarse_rsem, send, recv, pair_ssem, pair_rsem,
    gz_ssem, gz_rsem, gy_ssem, gy_rsem, gc_ssem, gc_rsem, nb_ssem, nb_rsem,
):
    j = lax.axis_index("cluster")
    s = lax.axis_index("sub")
    y = j // NZ
    z = j % NZ
    x = s // 2
    core = s % 2
    other = s + 1 - 2 * core
    face = y * NX + x
    place = face * NZ + z

    def chain(d):
        return ((j + d + CHAIN) % CHAIN, s)

    def beside(d):
        return ((j + d + CHAIN) % CHAIN, other)

    ys = [((y + d) % NY) * NZ for d in range(NY)]
    zs = [(z + d) % NZ for d in range(NZ)]
    xs = [((x + d) % NX) * 2 + core for d in range(NX)]

    def peer(dy, dx, dz):
        return (ys[dy] + zs[dz], xs[dx])

    barrier = pltpu.get_barrier_semaphore()

    def greet(device):
        pl.semaphore_signal(barrier, inc=1, device_id=device, device_id_type=MESH)

    for dz in (4, 3, 5, 2, 6, 1, 7):
        greet(peer(0, 0, dz))
    for d in (-2, 2, -1, 1):
        greet(chain(d))
        greet(beside(d))
    for dy, dx in FACES:
        greet(peer(dy, dx, 0))
    greet(beside(0))

    loads = [
        pltpu.make_async_copy(src, dst, load_sem.at[k])
        for k, (src, dst) in enumerate(
            (
                (loads_hbm, loads_ref), (count_hbm, count_ref), (modes_hbm, modes_ref),
                (order_hbm, order_ref), (coarse_hbm, coarse_ref), (schur_hbm, schur_ref),
                (right_hbm, right_ref), (scale_hbm, scale_ref),
            )
        )
    ]
    for copy in loads:
        copy.start()
    for copy in loads[:4]:
        copy.wait()

    count = count_ref[...]
    active = jnp.where(iota((MODES, 1), 0) < count, 1.0, 0.0)
    basis = modes_ref[:, 0, :] * active
    sub8 = iota((8, 128), 0)
    tmp_ref[...] = jnp.zeros((8, 128), F32)
    tmp_ref[0:MODES, 0:CASES] = loads_ref[:, 0, :] * active
    spread = fold_lanes(tmp_ref[...])
    own_loads = jnp.sum(
        jnp.where(iota((8, 128), 1) // CASES == sub8, spread, 0.0), axis=0, keepdims=True
    )
    out_ref[0] = jnp.concatenate([own_loads, jnp.zeros((1, 128), F32)], axis=0)

    hot = jnp.where(iota((M, M), 0) == order_ref[...], 1.0, 0.0).astype(BF16)
    bh, bl = parts(basis[:, :M])
    permuted = -(mul(bh, hot, NT) + mul(bl, hot, NT))
    left_out[...] = jnp.concatenate([permuted, jnp.zeros((2, M), F32)], axis=0)
    right_out[...] = jnp.concatenate([basis[:, M:], jnp.zeros((2, M), F32)], axis=0)

    loads[4].wait()
    chip = iota((NC, 128), 1)
    wanted = (chip // 32) * 384 + (chip % NZ) * 48 + (chip // NZ % NX) * 12
    pick = jnp.where(iota((NC, 128), 0) == wanted, 1.0, 0.0).astype(BF16)
    rows = jnp.concatenate([coarse_ref[...], jnp.zeros((2, NC), F32)], axis=0)
    for c in range(2):
        shifted = []
        for m in range(MODES):
            d = c * MODES + m
            shifted.append(rows if d == 0 else pltpu.roll(rows, NC - d, 1))
        high, low = parts(jnp.concatenate(shifted, axis=0))
        cp_ref[c] = mul(high, pick) + mul(low, pick)

    pl.semaphore_wait(barrier, 31)

    def remote(src, dst, ssem, rsem, device):
        return pltpu.make_async_remote_copy(
            src_ref=src, dst_ref=dst, send_sem=ssem, recv_sem=rsem,
            device_id=device, device_id_type=MESH,
        )

    def neighbour(k, src, dst, d):
        return remote(src, dst, nb_ssem.at[k], nb_rsem.at[k], chain(d))

    def all_wait(ref, count, sem):
        w = ref.at[pl.ds(0, count)]
        pltpu.make_async_copy(w, w, sem).wait()

    line = pl.ds(pl.multiple_of(2 * z, 2), 2)
    for dz in (4, 3, 5, 2, 6, 1, 7):
        remote(out_ref.at[0], line_ref.at[line], line_sems.at[0], line_sems.at[1], peer(0, 0, dz)).start()
    line_ref[line] = out_ref[0]

    left_copy = neighbour(0, left_out, left_in, -1)
    left_copy.start()
    right_copy = neighbour(1, right_out, right_in, 1)
    right_copy.start()
    colour = j % 4
    coarse_copies = []
    for k, d in enumerate((1, -1, -2)):
        coarse_copies.append(
            remote(cp_ref.at[core], crow_ref.at[0, colour], coarse_ssem.at[k], coarse_rsem.at[k], chain(d))
        )
    for k, d in enumerate((1, 0, -1, -2)):
        coarse_copies.append(
            remote(
                cp_ref.at[1 - core], crow_ref.at[1, colour], coarse_ssem.at[3 + k],
                coarse_rsem.at[3 + k], beside(d),
            )
        )

    for copy in coarse_copies:
        copy.start()
    crow_ref[0, colour] = cp_ref[core]

    for copy in loads[5:]:
        copy.wait()

    def split_rows(i, c):
        rows = pl.ds(pl.multiple_of(i * 128, 128), 128)
        high, low = parts(schur_ref[rows, :])
        sh_ref[rows, :] = high
        sl_ref[rows, :] = low
        for ref, part in ((sh_ref, high), (sl_ref, low)):
            ref[rows, 0:M] = (-mul(part[:, :M], hot, NT)).astype(BF16)
        return c

    def split_columns(i, c):
        cols = pl.ds(pl.multiple_of(i * 128, 128), 128)
        for ref in (sh_ref, sl_ref):
            ref[0:M, cols] = (-mul(hot, ref[0:M, cols])).astype(BF16)
        return c

    lax.fori_loop(0, 6, split_rows, 0)
    all_wait(line_ref, 14, line_sems.at[1])
    block = pl.ds(pl.multiple_of(16 * face, 16), 16)
    for dy, dx in FACES:
        remote(line_ref, in_ref.at[0, block], send.at[0], recv.at[0], peer(dy, dx, 0)).start()
    in_ref[0, block] = line_ref[...]
    lax.fori_loop(0, 6, split_columns, 0)

    landing = pl.ds(pl.multiple_of(2 * place, 2), 2)

    def start_send(r, dy, dx, dz):
        remote(out_ref.at[r], in_ref.at[r, landing], send.at[r], recv.at[r], peer(dy, dx, dz)).start()

    def send_own(r):
        in_ref[r, landing] = out_ref[r]

    def send_some(r, offsets):
        for offset in offsets:
            start_send(r, *offset)

    def send_all(r):
        send_some(r, OFFSETS)
        send_own(r)


    first = j > 0
    last = j < CHAIN - 1

    def apply_product(before, own):
        lifted = jnp.concatenate([jnp.where(first, before, 0.0), own], axis=1)
        return mulw(lifted, sh_ref[...], sl_ref[...])

    def apply_send(i, values):
        fwd[i] = values
        copy = neighbour(3 + 2 * i, fwd.at[i], fwd_in.at[i], 1)
        copy.start()
        return copy

    def apply_middle(i, copy, values):
        copy.wait_recv()
        image = apply_product(fwd_in[i], values)
        back[i] = image[:, :M]
        copy_back = neighbour(4 + 2 * i, back.at[i], back_in.at[i], -1)
        copy_back.start()
        return copy_back, image[:, M:]

    def apply_end(i, copy_back, own):
        copy_back.wait_recv()
        return own + jnp.where(last, back_in[i], 0.0)

    left_copy.wait_recv()
    right_copy.wait_recv()
    following = jnp.where(last, left_in[...], 0.0)
    here = pl.ds(pl.multiple_of(colour * 8, 8), 8)
    after = pl.ds(pl.multiple_of(((j + 1) % 4) * 8, 8), 8)
    ahead = pl.ds(pl.multiple_of(((j + 3) % 4) * 8, 8), 8)
    xa_ref[...] = jnp.zeros((32, 768), F32)
    xa_ref[here, 0:M] = right_out[...]
    xa_ref[after, 0:M] = following
    xa_ref[here, M:] = left_out[...]
    xa_ref[ahead, M:] = right_in[...]
    wide_image = apply_product(xa_ref[:, M:], xa_ref[:, 0:M])
    wide_back[...] = wide_image[:, :M]
    wide_copy = neighbour(2, wide_back, wide_back_in, -1)
    wide_copy.start()
    xa_ref[:, M:] = wide_image[:, M:]

    pieces = []
    for block in (right_out[...], following):
        for m in range(MODES):
            pieces.append(jnp.broadcast_to(block[m : m + 1, :], (CASES, M)))
        pieces.append(jnp.zeros((32, M), F32))
    wh, wl = parts(jnp.transpose(jnp.concatenate(pieces, axis=0)))
    wh_ref[...] = wh
    wl_ref[...] = wl

    for copy in coarse_copies:
        copy.wait_recv()
    ch, cl = parts(crow_ref[...].reshape(384, 128))
    column = iota((128, 256), 1)
    chip = column // 2
    spread = chip + (column % 2) * jnp.where(chip % NZ == NZ - 1, 25, 1)
    both = jnp.where(iota((128, 256), 0) == spread, 1.0, 0.0).astype(BF16)
    ch_ref[...] = mul(ch, both).astype(BF16)
    cl_ref[...] = mul(cl, both).astype(BF16)

    own_case = (iota((CASES, 256), 1) % CASES) == iota((CASES, 256), 0)
    slot = iota((MODES, 8, 128), 2) // CASES == iota((MODES, 8, 128), 0)

    def coefficients(r, field):
        product = mulw(field, wh_ref[...], wl_ref[...])
        flat = jnp.sum(jnp.where(own_case, product, 0.0), axis=0, keepdims=True)
        out_ref[r] = jnp.concatenate([flat[:, :128], flat[:, 128:]], axis=0)

    def picked(full, at):
        blocks = [
            jnp.sum(
                jnp.where(slot, full[at + c * 48 : at + (c + 1) * 48].reshape(MODES, 8, 128), 0.0),
                axis=0,
            )
            for c in range(4)
        ]
        return jnp.concatenate(blocks, axis=0)

    def coarse(r):
        all_wait(in_ref.at[r], 254 if r else 240, recv.at[r])
        gh, gl = parts(in_ref[r])
        both = mul(ch_ref[...], jnp.concatenate([gh, gl], axis=1))
        full = both[:, :128] + both[:, 128:] + mul(cl_ref[...], gh)
        pair_out[r] = picked(full, 192)
        copy = remote(pair_out.at[r], pair_in.at[r], pair_ssem.at[r], pair_rsem.at[r], beside(0))
        copy.start()
        mine = picked(full, 0)
        copy.wait_recv()
        turned = jnp.transpose(mine + pair_in[r])
        return jnp.sum(turned.reshape(8, CASES, 32), axis=0)

    def grams(a, blocks):
        spare = jnp.zeros((128 - CASES * len(blocks), M), F32)
        return mul3(a, jnp.concatenate([*blocks, spare], axis=0), NT)

    def gram_z(i, values):
        gz_out[i] = values
        for dz in (4, 3, 5, 2, 6, 1, 7):
            remote(gz_out.at[i], gz_in.at[i, z], gz_ssem.at[i], gz_rsem.at[i], peer(0, 0, dz)).start()
        gz_in[i, z] = values

    def gram_y(i):
        all_wait(gz_in.at[i], NZ - 1, gz_rsem.at[i])
        values = jnp.sum(gz_in[i], axis=0)
        gy_out[i] = values
        for dy, dx in FACES:
            remote(
                gy_out.at[i], gy_in.at[i, face], gy_ssem.at[i], gy_rsem.at[i], peer(dy, dx, 0)
            ).start()
        gy_in[i, face] = values

    def gram_pair(i):
        all_wait(gy_in.at[i], NY * NX - 1, gy_rsem.at[i])
        values = jnp.sum(gy_in[i], axis=0)
        gc_out[i] = values
        copy = remote(gc_out.at[i], gc_in.at[i], gc_ssem.at[i], gc_rsem.at[i], beside(0))
        copy.start()
        return copy, values

    def gram_end(i, copy, values):
        copy.wait_recv()
        return values + gc_in[i]

    right = right_ref[...]
    scale = scale_ref[...]
    y0 = coarse(0)
    wide_copy.wait_recv()
    xa_ref[:, M:] = xa_ref[:, M:] + jnp.where(last, wide_back_in[...], 0.0)
    moved = mul3(y0, xa_ref[...])
    mult = moved[:, :M]
    tt = right - moved[:, M:]

    coefficients(1, tt)
    send_all(1)
    resid = tt - mul3(coarse(1), xa_ref[:, 0:M])
    scaled = scale * resid

    coefficients(2, scaled)
    copy = apply_send(0, scaled)
    send_all(2)
    copy_back, own = apply_middle(0, copy, scaled)
    y2 = coarse(2)
    p = apply_end(0, copy_back, own)
    moved = mul3(y2, xa_ref[...])
    a = scaled - moved[:, :M]
    p = p - moved[:, M:]

    coefficients(3, p)
    send_all(3)
    q = p - mul3(coarse(3), xa_ref[:, 0:M])
    scaled = scale * q

    coefficients(4, scaled)
    copy = apply_send(1, scaled)
    send_all(4)
    gram_z(0, grams(a, (p, resid, q)))
    copy_back, own = apply_middle(1, copy, scaled)
    y4 = coarse(4)
    u = apply_end(1, copy_back, own)
    moved = mul3(y4, xa_ref[...])
    w = scaled - moved[:, :M]
    u = u - moved[:, M:]

    gram_z(1, grams(w, (p, u, resid, q)))
    coefficients(5, u)
    send_some(5, OFFSETS[:48])
    gram_y(0)
    send_some(5, OFFSETS[48:100])
    gram_y(1)
    send_some(5, OFFSETS[100:])
    send_own(5)
    copy, values = gram_pair(0)
    sums = gram_end(0, copy, values)
    ap, ar, aq = (sums[:, k * CASES : (k + 1) * CASES] for k in range(3))
    eye = jnp.where(iota((CASES, CASES), 0) == iota((CASES, CASES), 1), 1.0, 0.0)
    inverse = eliminate(ap, eye)
    alpha = exact(inverse, ar)
    rest = ar - exact(aq, alpha)
    v = u - mul3(coarse(5), xa_ref[:, 0:M])
    aq_fields = jnp.concatenate([a, q], axis=1)
    first_step = exact(alpha, aq_fields, TN)
    copy, values = gram_pair(1)
    sums = gram_end(1, copy, values)
    wp, wu, wr, wq = (sums[:, k * CASES : (k + 1) * CASES] for k in range(4))
    across = exact(inverse, wp, NT)
    right_side = wr - exact(wq, alpha) - exact(across, rest, TN)
    gamma = eliminate(wu - exact(wp, across), right_side)
    turned = jnp.concatenate([w, v], axis=1) - exact(across, aq_fields, TN)
    mixed = first_step + exact(gamma, turned, TN)
    both_ref[0:CASES] = mult + mixed[:, :M]
    both_ref[CASES:] = resid - mixed[:, M:]

    left_copy.wait_send()
    right_copy.wait_send()
    all_wait(line_ref, 14, line_sems.at[0])
    for copy in coarse_copies:
        copy.wait_send()
    pltpu.make_async_copy(wide_back, wide_back, nb_ssem.at[2]).wait()
    for i in range(2):
        pltpu.make_async_copy(fwd.at[i], fwd.at[i], nb_ssem.at[3 + 2 * i]).wait()
        pltpu.make_async_copy(back.at[i], back.at[i], nb_ssem.at[4 + 2 * i]).wait()
        all_wait(gz_in.at[i], NZ - 1, gz_ssem.at[i])
        all_wait(gy_in.at[i], NY * NX - 1, gy_ssem.at[i])
        pltpu.make_async_copy(gc_out.at[i], gc_out.at[i], gc_ssem.at[i]).wait()
    for r in range(6):
        all_wait(in_ref.at[r], 254 if r else 240, send.at[r])
        pltpu.make_async_copy(pair_out.at[r], pair_out.at[r], pair_ssem.at[r]).wait()


def shards(right, schur, modes, count, order, scale, loads, coarse):
    vmem = pl.BlockSpec(memory_space=pltpu.VMEM)
    dma = pltpu.SemaphoreType.DMA
    v = pltpu.VMEM
    both = pl.pallas_call(
        kernel,
        name="feti",
        out_shape=jax.ShapeDtypeStruct((2 * CASES, M), F32),
        in_specs=[pl.BlockSpec(memory_space=pltpu.HBM)] * 8,
        out_specs=vmem,
        scratch_shapes=[
            v((CASES, M), F32), v((MODES, 1, 768), F32), v((1, 1), jnp.int32), v((1, M), jnp.int32),
            v((1, M), F32), v((MODES, 1, CASES), F32), v((MODES, NC), F32),
            v((768, 768), F32), v((768, 768), BF16), v((768, 768), BF16),
            v((M, 256), BF16), v((M, 256), BF16), v((32, 768), F32),
            v((2, 48, 128), F32), v((2, 4, 48, 128), F32), v((384, 256), BF16), v((384, 256), BF16),
            v((6, 2, 128), F32), v((6, 256, 128), F32), v((6, 32, 128), F32), v((6, 32, 128), F32),
            v((2, 16, 128), F32), v((2, NZ, 16, 128), F32),
            v((2, 16, 128), F32), v((2, NY * NX, 16, 128), F32),
            v((2, 16, 128), F32), v((2, 16, 128), F32),
            v((8, M), F32), v((8, M), F32), v((8, M), F32), v((8, M), F32),
            v((2, 16, M), F32), v((2, 16, M), F32), v((32, M), F32), v((32, M), F32),
            v((2, 16, M), F32), v((2, 16, M), F32),
            v((8, 128), F32), v((16, 128), F32),
            dma((8,)), dma((2,)), dma((7,)), dma((7,)), dma((6,)), dma((6,)), dma((6,)), dma((6,)),
            dma((2,)), dma((2,)), dma((2,)), dma((2,)), dma((2,)), dma((2,)), dma((7,)), dma((7,)),
        ],
        compiler_params=pltpu.CompilerParams(
            collective_id=0, has_side_effects=True, vmem_limit_bytes=60 * 1024 * 1024
        ),
    )(
        right.reshape(CASES, M), schur.reshape(768, 768), modes.reshape(MODES, 1, 768), count,
        order.reshape(1, M), scale.reshape(1, M), loads.reshape(MODES, 1, CASES), coarse,
    )
    return both[:CASES].reshape(1, 1, CASES, M), both[CASES:].reshape(1, 1, CASES, M)


def solution(mesh):
    field = P("sub", "cluster", None, None)
    return jax.shard_map(
        shards,
        mesh=mesh,
        in_specs=(
            field, field, field, P("sub", "cluster"), P("sub", "cluster", None),
            P("sub", "cluster", None), field, P(("cluster", "sub"), None),
        ),
        out_specs=(field, field),
        check_vma=False,
    )
```
